32 devices in a mesh: dp: 8 (over z, x), expert: 4 (over y, core).
Axes of the slice: x: 2, y: 2, z: 4, core: 2. Of those that a mesh axis runs over, the one named last changes fastest.
Arguments:
- activations: bfloat16 [4096, 6144], P(('dp', 'expert')), may hold values from -6 to 6
- gate_gradient: bfloat16 [4096, 2, 8192], P(('dp', 'expert')), may hold values from -0.1796875 to 0.1796875
- routes: int32 [4096, 2], P(('dp', 'expert')), may hold values from 0 to 3, as said below
- sequence_ids: int32 [32, 128], P(('dp', 'expert')), may hold values from 0 to 3, never falling along the last dimension, each value on 1 to 64 neighbouring positions
- input_basis: bfloat16 [4, 6144, 6144], P('expert', None, 'dp'), may hold values from -0.109375 to 0.109375
- output_basis: bfloat16 [4, 8192, 8192], P('expert', None, 'dp'), may hold values from -0.09375 to 0.09375
- input_query: bfloat16 [4, 6144, 128], P('expert', 'dp'), may hold values from -0.078125 to 0.078125
- output_query: bfloat16 [4, 8192, 128], P('expert', 'dp'), may hold values from -0.0625 to 0.0625
Outputs:
- scores: float32 [128, 4], P(('dp', 'expert'))
The draws below stay inside these ranges and needn't reach their ends.
Inputs may be any that keep to these rules, and one draw needn't show every extreme that they name: `routes`: each token names 2 different experts. Among the 128 tokens of one aligned block (the rows of one device) no expert is named more than 128 times, and in every block one expert is named exactly 128 times, the same expert in all blocks of an aligned group of 4 consecutive blocks.
All inputs are finite; a program needn't handle non-finite values.
Results may differ from the reference program's by a relative error of at most 0.004.
Values may be sent and summed in bfloat16 or wider, within the bound.
No kernel may reach another device: no remote copies, remote signals or barrier semaphores. Data moves between devices by JAX's collectives and lax.ppermute only.
A program may use at most 128 MiB of HBM per device.

```python
import math
import jax
import jax.numpy as jnp
import numpy as np
from jax import lax

D = 6144
FF = 8192
TOP = 2
RANK = 32
NQ = 4
TOK_DEV = 128
SEG_DEV = 4
SEQ_MOST = 64
EXPERTS = 4
CAP = 128
QR = 128
BLOCKS = 32
TOKENS = 4096
SEQS = 128


def route_table(key):
    block_count = TOKENS // TOK_DEV
    per_block = TOK_DEV * TOP
    key_busy, key_order, key_token, key_swap = jax.random.split(key, 4)
    busy_row = jax.random.randint(key_busy, (block_count // EXPERTS,), 0, EXPERTS)
    busy = jnp.repeat(busy_row, EXPERTS)
    expert_ids = jnp.arange(EXPERTS, dtype=jnp.int32)
    priority = jax.random.randint(key_order, (block_count, EXPERTS), 0, 1 << 20) * EXPERTS + expert_ids[None, :]
    priority = jnp.where(expert_ids[None, :] == busy[:, None], -1, priority)
    order = jnp.argsort(priority, axis=1).astype(jnp.int32)
    remain = per_block - CAP
    base = remain // (EXPERTS - 1)
    extra = remain % (EXPERTS - 1)
    counts = jnp.where(expert_ids == 0, CAP, base + (expert_ids - 1 < extra).astype(jnp.int32))
    ends = jnp.cumsum(counts)
    position = jnp.arange(per_block, dtype=jnp.int32)
    group = jnp.sum((position[:, None] >= ends[None, :]).astype(jnp.int32), axis=1)
    labels = order[:, group]
    token_ids = jnp.arange(TOK_DEV, dtype=jnp.int32)
    shuffle = jnp.argsort(jax.random.randint(key_token, (block_count, TOK_DEV), 0, 1 << 20) * TOK_DEV + token_ids[None, :], axis=1).astype(jnp.int32)
    first = jnp.take_along_axis(labels, shuffle, axis=1)
    second = jnp.take_along_axis(labels, shuffle + TOK_DEV, axis=1)
    swapped = jax.random.randint(key_swap, (block_count, TOK_DEV), 0, 2) == 1
    lead = jnp.where(swapped, second, first)
    trail = jnp.where(swapped, first, second)
    return jnp.stack([lead, trail], axis=-1).reshape(TOKENS, TOP).astype(jnp.int32)


def draw_routes(key, part):
    return route_table(key)


def with_spikes(array, stream_key, source, target, parts, factor):
    def block_of(dim):
        return (jnp.arange(array.shape[dim]) // (array.shape[dim] // parts)).reshape((-1,) + (1,) * (array.ndim - 1 - dim))

    first = jax.random.permutation(stream_key, parts)[block_of(target)]
    second = (block_of(target) + parts // 2) % parts
    return jnp.where((block_of(source) == first) | (block_of(source) == second), factor * array, array)


def shard_levels(stream_key, dims, cuts, smallest, high):
    factor_of, own = 1.0, jax.random.fold_in(stream_key, 6)
    for dim, parts in cuts:
        draws = jnp.exp(jax.random.uniform(jax.random.fold_in(own, dim), (parts,), jnp.float32, smallest / len(cuts), high / len(cuts)))
        factor_of = factor_of * jnp.repeat(draws, dims[dim] // parts).reshape([-1 if axis == dim else 1 for axis in range(len(dims))])
    return factor_of


def split_up(number_of, total, reach, skew):
    loads = [(1 << 20) // math.isqrt(rank ** skew) + 1 for rank in range(2, number_of + 1)]
    rest, given = total - reach - (number_of - 1), [1] * (number_of - 1)
    while rest > 0:
        movable = [i for i in range(number_of - 1) if given[i] < reach]
        pool, budget = sum([loads[i] for i in movable]), rest
        for i in movable:
            more = min(reach - given[i], max(1, budget * loads[i] // pool), rest)
            given[i] = given[i] + more
            rest = rest - more
    return np.array([reach] + given)


def ragged_sizes(key, count, total, limit, skew):
    if count == 2:
        one = jax.random.randint(key, (), max(1, total - limit), min(limit, total - 1) + 1)
        return jnp.stack([one, total - one])
    tallies = jnp.asarray(split_up(count, total, limit, skew), jnp.int32)
    couples = (count - 1) // 2
    donor, receiver = tallies[1:1 + 2 * couples:2], tallies[2:2 + 2 * couples:2]
    room = jnp.minimum(donor - 1, limit - receiver)
    shifted = jax.random.randint(jax.random.fold_in(key, 1), (couples,), 0, 1 << 20) % (room + 1)
    tallies = tallies.at[1:1 + 2 * couples:2].set(donor - shifted).at[2:2 + 2 * couples:2].set(receiver + shifted)
    return tallies[jax.random.permutation(jax.random.fold_in(key, 2), count)]


def bell_draw(rng, dims, deviation, limit, shards=(), kind=jnp.bfloat16):
    array = jax.random.normal(rng, dims, jnp.float32) * deviation
    if len(shards) > 0:
        array = shard_levels(rng, dims, shards, -0.22, 0.18) * array
    return jnp.clip(array, min=-limit, max=limit).astype(kind)


def gaussian_with(rng, shape, scale, limit, cuts, heavy, kind=jnp.bfloat16):
    array = scale * jax.random.normal(rng, shape, jnp.float32)
    if cuts:
        array = array * shard_levels(rng, shape, cuts, -0.22, 0.18)
    return jnp.clip(with_spikes(array, jax.random.fold_in(rng, 3), *heavy), -limit, limit).astype(kind)


def setup_inputs(seed: int = 0) -> dict:
    seeds = jax.random.split(jax.random.key(seed), 9)
    activations = bell_draw(seeds[0], (TOKENS, D), 1.0, 6.0, ((0, 32),))
    gate_gradient = bell_draw(seeds[1], (TOKENS, TOP, FF), 0.03, 0.1796875, ((0, 32),))
    routes = draw_routes(jax.random.fold_in(seeds[8], 71), 0)
    sequence_ids = jax.vmap(lambda own: jnp.searchsorted(jnp.cumsum(ragged_sizes(own, SEG_DEV, TOK_DEV, SEQ_MOST, 2)), jnp.arange(TOK_DEV), side="right"))(jax.random.split(seeds[3], BLOCKS)).reshape((BLOCKS, TOK_DEV)).astype(jnp.int32)
    input_basis = gaussian_with(seeds[4], (EXPERTS, D, D), D ** -0.5, 0.109375, ((0, 4), (2, 8)), (2, 1, 8, 2.0))
    output_basis = gaussian_with(seeds[5], (EXPERTS, FF, FF), FF ** -0.5, 0.09375, ((0, 4), (2, 8)), (2, 1, 8, 2.0))
    input_query = bell_draw(seeds[6], (EXPERTS, D, QR), D ** -0.5, 0.078125, ((0, 4), (1, 8)))
    output_query = bell_draw(seeds[7], (EXPERTS, FF, QR), FF ** -0.5, 0.0625, ((0, 4), (1, 8)))
    return {"activations": activations, "gate_gradient": gate_gradient, "routes": routes, "sequence_ids": sequence_ids, "input_basis": input_basis, "output_basis": output_basis, "input_query": input_query, "output_query": output_query}


def fold_pair(pair):
    return jnp.dot(pair[0], pair[1], preferred_element_type=jnp.float32).astype(jnp.bfloat16)


def reference(activations, gate_gradient, routes, sequence_ids, input_basis, output_basis, input_query, output_query):
    fold_input = lax.map(fold_pair, (input_basis, input_query))
    fold_output = lax.map(fold_pair, (output_basis, output_query))
    flat_gradient = gate_gradient.reshape(TOKENS * TOP, FF)
    flat_routes = routes.reshape(TOKENS * TOP)

    def per_expert(carry, expert):
        input_terms = jnp.dot(activations, fold_input[expert], preferred_element_type=jnp.float32)
        input_terms = jnp.repeat(input_terms, TOP, axis=0)
        output_terms = jnp.dot(flat_gradient, fold_output[expert], preferred_element_type=jnp.float32)
        product = (input_terms * output_terms).reshape(TOKENS * TOP, NQ, RANK).sum(axis=-1)
        chosen = (flat_routes == expert)[:, None]
        return carry + jnp.where(chosen, product, jnp.zeros((), jnp.float32)), None

    start_value = jnp.zeros((TOKENS * TOP, NQ), jnp.float32)
    route_scores, _ = lax.scan(per_expert, start_value, jnp.arange(EXPERTS, dtype=jnp.int32))
    token_scores = route_scores.reshape(TOKENS, TOP, NQ).sum(axis=1).reshape(BLOCKS, TOK_DEV, NQ)
    membership = (sequence_ids[:, :, None] == jnp.arange(SEG_DEV, dtype=jnp.int32)[None, None, :]).astype(jnp.float32)
    scores = jnp.einsum("bts,btq->bsq", membership, token_scores, precision=lax.Precision.HIGHEST)
    return scores.reshape(SEQS, NQ)
```

```python
import jax
import jax.numpy as jnp
from jax import lax
from jax.experimental import pallas as pl
from jax.experimental.pallas import tpu as pltpu
from jax.sharding import PartitionSpec as P

RANK = 32
SEG_DEV = 4
CORES = 2
TOP_EXPONENT = 15.0
TAIL = 16


def bits_of(count):
    return (count - 1).bit_length()


def slot_order(order):
    width = len(order)
    return [
        sum(((slot >> (width - 1 - i)) & 1) << bit for i, bit in enumerate(order))
        for slot in range(1 << width)
    ]


def fold_kernel(table_ref, basis_ref, query_ref, out_ref):
    out_ref[...] = jnp.dot(
        basis_ref[...], query_ref[...], preferred_element_type=jnp.float32
    )


def fold_part(basis, query, table, rows):
    depth, columns = query.shape
    blocks = table.shape[0]
    return pl.pallas_call(
        fold_kernel,
        grid_spec=pltpu.PrefetchScalarGridSpec(
            num_scalar_prefetch=1,
            grid=(blocks,),
            in_specs=[
                pl.BlockSpec((rows, depth), lambda i, t: (t[i], 0)),
                pl.BlockSpec((depth, columns), lambda i, t: (0, 0)),
            ],
            out_specs=pl.BlockSpec((rows, columns), lambda i, t: (i, 0)),
        ),
        out_shape=jax.ShapeDtypeStruct((blocks * rows, columns), jnp.float32),
        compiler_params=pltpu.CompilerParams(vmem_limit_bytes=24 * 1024 * 1024),
        cost_estimate=pl.CostEstimate(
            flops=2 * blocks * rows * depth * columns,
            bytes_accessed=blocks * rows * (depth * 2 + columns * 4),
            transcendentals=0,
        ),
    )(table, basis, query)


def column_exponent(query):
    peak = jnp.max(jnp.abs(query), axis=0, keepdims=True).astype(jnp.float32)
    bound = jnp.maximum(peak * (0.25 * query.shape[0]), 1e-28)
    return jnp.floor(jnp.log2(bound)) + 1.0


def pack(values, exponent):
    scaled = values * jnp.exp2(TOP_EXPONENT - exponent)
    tail = jnp.broadcast_to(exponent, (TAIL, values.shape[1]))
    return jnp.concatenate([scaled, tail], axis=0).astype(jnp.float16)


def unpack(packed):
    rows = packed.shape[0] - TAIL
    exponent = packed[rows : rows + 1].astype(jnp.float32)
    return packed[:rows].astype(jnp.float32) * jnp.exp2(exponent - TOP_EXPONENT), exponent


def flip(size, mask):
    return [(i, i ^ mask) for i in range(size)]


def reduce_parts(keep, send, exponent, order, blocks):
    for stage, bit in enumerate(order):
        landed = lax.ppermute(pack(send, exponent), "dp", flip(blocks, 1 << bit))
        values, other = unpack(landed)
        total = keep + values
        exponent = jnp.maximum(exponent, other) + 1.0
        if stage + 1 < len(order):
            half = total.shape[0] // 2
            keep, send = total[:half], total[half:]
    return total


def per_device(
    activations,
    gate_gradient,
    routes,
    sequence_ids,
    input_basis,
    output_basis,
    input_query,
    output_query,
):
    blocks = lax.axis_size("dp")
    group = lax.axis_size("expert")
    halves = group // CORES
    place = lax.axis_index("dp")
    member = lax.axis_index("expert")
    half = member // CORES
    core = member % CORES
    tokens, top = routes.shape
    columns = input_query.shape[2]
    queries = columns // RANK
    count = bits_of(blocks)

    def folded(basis, query, order):
        rows = basis.shape[0] // (blocks * halves)
        slots = jnp.array(slot_order(order), jnp.int32) ^ place
        parts = jnp.arange(halves, dtype=jnp.int32) ^ half
        table = (parts[None, :] * blocks + slots[:, None]).reshape(-1)
        middle = table.shape[0] // 2
        exponent = column_exponent(query)
        send = fold_part(basis, query, table[middle:], rows)
        keep = fold_part(basis, query, table[:middle], rows)
        total = reduce_parts(keep, send, exponent, order, blocks)
        shard = total.astype(jnp.bfloat16).reshape(halves, rows, columns)
        pieces = [shard[0]] + [
            lax.ppermute(shard[d], "expert", flip(group, d * CORES))
            for d in range(1, halves)
        ]
        return lax.all_gather(jnp.concatenate(pieces, axis=1), "dp", axis=0, tiled=True)

    def gathered(array):
        parts = array.reshape(array.shape[0], halves, -1)
        mine = [
            lax.dynamic_index_in_dim(parts, half ^ d, axis=1, keepdims=False)
            for d in range(halves)
        ]
        mine = [
            block if d == 0 else lax.ppermute(block, "expert", flip(group, d * CORES))
            for d, block in enumerate(mine)
        ]
        landed = []
        for block in mine:
            landed.append(block)
            landed.append(lax.ppermute(block, "expert", flip(group, 1)))
        return jnp.concatenate(landed, axis=0)

    fold_input = folded(input_basis[0], input_query[0], list(range(count)))
    fold_output = folded(
        output_basis[0], output_query[0], [(i + 1) % count for i in range(count)]
    )
    group_inputs = gathered(activations)
    group_gradient = [gathered(gate_gradient[:, k]) for k in range(top)]

    small = jnp.concatenate([routes.T, sequence_ids], axis=0)
    small = lax.all_gather(small, "expert", axis=0)
    small = small[member ^ jnp.arange(group, dtype=jnp.int32)]
    group_routes = [small[:, k].reshape(-1) for k in range(top)]
    group_sequences = small[:, top]

    expert_of = [(half ^ d) * CORES + core for d in range(halves)]

    def chosen(terms, route):
        out = jnp.zeros((terms.shape[0], columns), jnp.float32)
        for d in range(halves):
            hit = (route == expert_of[d])[:, None]
            out = out + jnp.where(hit, terms[:, d * columns : (d + 1) * columns], 0.0)
        return out

    input_terms = jnp.dot(group_inputs, fold_input, preferred_element_type=jnp.float32)
    input_chosen = jnp.stack([chosen(input_terms, route) for route in group_routes])
    for bit in range(bits_of(halves)):
        landed = lax.ppermute(
            input_chosen, "expert", flip(group, CORES << bit)
        ).reshape(top, halves, CORES * tokens, columns)
        order = [d ^ (1 << bit) for d in range(halves)]
        landed = jnp.concatenate([landed[:, d : d + 1] for d in order], axis=1)
        input_chosen = input_chosen + landed.reshape(input_chosen.shape)

    token_products = jnp.zeros((group * tokens, columns), jnp.float32)
    for k in range(top):
        output_terms = jnp.dot(
            group_gradient[k], fold_output, preferred_element_type=jnp.float32
        )
        token_products = token_products + input_chosen[k] * chosen(output_terms, group_routes[k])
    token_scores = token_products.reshape(group, tokens, queries, RANK).sum(axis=-1)
    membership = (
        group_sequences[:, :, None] == jnp.arange(SEG_DEV, dtype=jnp.int32)[None, None, :]
    ).astype(jnp.float32)
    partial = jnp.einsum(
        "gts,gtq->gsq",
        membership,
        token_scores,
        precision=lax.Precision.HIGHEST,
        preferred_element_type=jnp.float32,
    )
    scores = partial[0]
    for d in range(1, group):
        scores = scores + lax.ppermute(partial[d], "expert", flip(group, d))
    return scores


def solution(mesh):
    return jax.shard_map(
        per_device,
        mesh=mesh,
        in_specs=(
            P(("dp", "expert"), None),
            P(("dp", "expert"), None, None),
            P(("dp", "expert"), None),
            P(("dp", "expert"), None),
            P("expert", None, "dp"),
            P("expert", None, "dp"),
            P("expert", "dp", None),
            P("expert", "dp", None),
        ),
        out_specs=P(("dp", "expert"), None),
        check_vma=False,
    )
```

```python
import functools

import jax
import jax.numpy as jnp
from jax import lax
from jax.experimental import pallas as pl
from jax.experimental.pallas import tpu as pltpu
from jax.sharding import PartitionSpec as P

RANK = 32
SEG_DEV = 4
CORES = 2
TOP_EXPONENT = 15.0


def bits_of(count):
    return (count - 1).bit_length()


def slot_order(order):
    width = len(order)
    return [
        sum(((slot >> (width - 1 - i)) & 1) << bit for i, bit in enumerate(order))
        for slot in range(1 << width)
    ]


def column_exponent(query):
    peak = jnp.max(jnp.abs(query).astype(jnp.float32), axis=0, keepdims=True)
    bound = jnp.maximum(peak * (0.25 * query.shape[0]), 1e-28)
    return jnp.floor(jnp.log2(bound)) + 1.0


def fold_kernel(steps, width, *refs):
    position_ref, *basis_refs, query_ref, exponent_ref, send_ref, keep_ref = refs
    step = pl.program_id(0)
    rows = basis_refs[0].shape[0]
    scale = jnp.exp2(TOP_EXPONENT - exponent_ref[0:1, :])

    def terms(part):
        return jnp.dot(
            basis_refs[part][...], query_ref[...], preferred_element_type=jnp.float32
        )

    @pl.when(step < steps // 2)
    def _():
        for part in range(width):
            send_ref[pl.ds(part * rows, rows), :] = terms(part) * scale

    @pl.when(step >= steps // 2)
    def _():
        for part in range(width):
            keep_ref[pl.ds(part * rows, rows), :] = terms(part)


def fold_partial(basis, query, exponent, position, order, halves):
    depth, columns = query.shape
    blocks = 1 << len(order)
    count = blocks * halves
    rows = basis.shape[0] // count
    width = min(4, count // 2)
    steps = count // width

    def block(part):
        def index(i, position_ref):
            slot = (i * width + part) // halves ^ (blocks // 2)
            relative = sum(
                ((slot >> (len(order) - 1 - n)) & 1) << bit for n, bit in enumerate(order)
            )
            here = (i * width + part) % halves ^ position_ref[1]
            return here * blocks + (relative ^ position_ref[0]), 0

        return pl.BlockSpec((rows, depth), index)

    out = jax.ShapeDtypeStruct((count // 2 * rows, columns), jnp.float32)
    return pl.pallas_call(
        functools.partial(fold_kernel, steps, width),
        grid_spec=pltpu.PrefetchScalarGridSpec(
            num_scalar_prefetch=1,
            grid=(steps,),
            in_specs=[block(part) for part in range(width)]
            + [
                pl.BlockSpec((depth, columns), lambda i, p: (0, 0)),
                pl.BlockSpec(exponent.shape, lambda i, p: (0, 0)),
            ],
            out_specs=[
                pl.BlockSpec(
                    (width * rows, columns), lambda i, p: (jnp.minimum(i, steps // 2 - 1), 0)
                ),
                pl.BlockSpec(
                    (width * rows, columns), lambda i, p: (jnp.maximum(i - steps // 2, 0), 0)
                ),
            ],
        ),
        out_shape=[out, out],
        compiler_params=pltpu.CompilerParams(vmem_limit_bytes=56 * 1024 * 1024),
        cost_estimate=pl.CostEstimate(
            flops=2 * basis.size * columns,
            bytes_accessed=2 * basis.size + 4 * basis.shape[0] * columns,
            transcendentals=0,
        ),
    )(position, *([basis] * width), query, exponent)


def pack(values, exponent):
    return (values * jnp.exp2(TOP_EXPONENT - exponent)).astype(jnp.float16)


def unpack(packed, exponent):
    return packed.astype(jnp.float32) * jnp.exp2(exponent - TOP_EXPONENT)


def flip(size, mask):
    return [(i, i ^ mask) for i in range(size)]


def tie(*values):
    return lax.optimization_barrier(values)


def start_all(copies, done):
    started = []
    for i, (source, target) in enumerate(copies):
        started.append(pltpu.make_async_copy(source, target, done.at[i]))
        started[i].start()
    return started


def input_kernel(top, fold_ref, mask_ref, *refs):
    *token_refs, out_ref, sent_ref, tokens_ref, held_ref, done = refs
    count = token_refs[0].shape[0]
    copies = [(fold_ref, held_ref)] + [
        (token_ref, tokens_ref.at[pl.ds(i * count, count), :])
        for i, token_ref in enumerate(token_refs)
    ]
    for copy in start_all(copies, done):
        copy.wait()
    terms = jnp.dot(tokens_ref[...], held_ref[...], preferred_element_type=jnp.float32)
    total = tokens_ref.shape[0]
    columns = out_ref.shape[1]
    for k in range(top):
        rows_of = pl.ds(k, total, stride=top)
        out_ref[rows_of, :] = sum(
            terms[:, d * columns : (d + 1) * columns] * mask_ref[d, rows_of, :]
            for d in range(mask_ref.shape[0])
        )
    sent_ref[...] = out_ref[...].astype(sent_ref.dtype)


def input_chosen(pieces, fold, mask, top):
    total = sum(piece.shape[0] for piece in pieces)
    width, across = fold.shape
    columns = mask.shape[2]
    return pl.pallas_call(
        functools.partial(input_kernel, top),
        in_specs=[pl.BlockSpec(memory_space=pl.ANY), pl.BlockSpec(memory_space=pltpu.VMEM)]
        + [pl.BlockSpec(memory_space=pl.ANY)] * len(pieces),
        out_specs=[pl.BlockSpec(memory_space=pltpu.VMEM)] * 2,
        out_shape=[
            jax.ShapeDtypeStruct((total * top, columns), jnp.float32),
            jax.ShapeDtypeStruct((total * top, columns), jnp.bfloat16),
        ],
        scratch_shapes=[
            pltpu.VMEM((total, width), pieces[0].dtype),
            pltpu.VMEM((width, across), fold.dtype),
            pltpu.SemaphoreType.DMA((len(pieces) + 1,)),
        ],
        compiler_params=pltpu.CompilerParams(vmem_limit_bytes=58 * 1024 * 1024),
        cost_estimate=pl.CostEstimate(
            flops=2 * total * width * across,
            bytes_accessed=2 * (total + across) * width,
            transcendentals=0,
        ),
    )(fold, mask, *pieces)


def score_kernel(
    counts, orders, parts, position_ref, mask_ref, member_ref, query_ref, chosen_ref, *refs
):
    *refs, out_ref, tokens_ref, fold_ref, total_ref, folded, done = refs
    token_refs, refs = refs[: len(counts)], refs[len(counts) :]
    held_refs, landed_refs = refs[: 2 * len(orders)], refs[2 * len(orders) :]
    width = fold_ref.shape[0] // parts
    columns = chosen_ref.shape[1]
    copies = []
    for n, order in enumerate(orders):
        slots, rows, _ = held_refs[2 * n].shape
        for slot, relative in enumerate(slot_order(order)):
            start = (relative ^ position_ref[0]) * (rows * len(orders)) + n * rows
            start = pl.multiple_of(start, rows)
            source = held_refs[2 * n + slot // slots].at[slot % slots]
            copies.append((source, fold_ref.at[pl.ds(start, rows), :]))
    fold_copies = start_all(copies, folded)
    started = []
    for part in range(parts):
        across = pl.ds(part * width, width)
        copies = []
        start = 0
        for count, token_ref in zip(counts, token_refs):
            copies.append((token_ref.at[:, across], tokens_ref.at[pl.ds(start, count), across]))
            start += count
        started.append(start_all(copies, done.at[part]))
    for copy in fold_copies:
        copy.wait()
    for part in range(parts):
        for copy in started[part]:
            copy.wait()
        across = pl.ds(part * width, width)
        terms = jnp.dot(
            tokens_ref[:, across], fold_ref[across, :], preferred_element_type=jnp.float32
        )
        total_ref[...] = terms if part == 0 else total_ref[...] + terms
    output = sum(
        total_ref[:, d * columns : (d + 1) * columns] * mask_ref[d]
        for d in range(mask_ref.shape[0])
    )
    halves = len(landed_refs) + 1
    rows = chosen_ref.shape[0] // halves
    summed = jnp.zeros((member_ref.shape[0], columns), jnp.float32)
    for h in range(halves):
        here = pl.ds(h * rows, rows)
        inputs = chosen_ref[here, :]
        for d, landed_ref in enumerate(landed_refs):
            landed = landed_ref[pl.ds((h ^ (d + 1)) * rows, rows), :]
            inputs = inputs + landed.astype(jnp.float32)
        summed = summed + jnp.dot(
            member_ref[:, here],
            inputs * output[h * rows : (h + 1) * rows],
            precision=lax.Precision.HIGHEST,
            preferred_element_type=jnp.float32,
        )
    out_ref[...] = jnp.dot(
        summed,
        query_ref[...],
        precision=lax.Precision.HIGHEST,
        preferred_element_type=jnp.float32,
    )


def partial_scores(
    pieces, held, orders, position, mask, membership, query_sum, chosen, landed
):
    counts = [piece.shape[0] for piece in pieces]
    total = sum(counts)
    width = pieces[0].shape[1]
    across = held[0].shape[2]
    parts = 4
    return pl.pallas_call(
        functools.partial(score_kernel, counts, orders, parts),
        in_specs=[pl.BlockSpec(memory_space=pltpu.SMEM)]
        + [pl.BlockSpec(memory_space=pltpu.VMEM)] * 4
        + [pl.BlockSpec(memory_space=pl.ANY)] * (len(pieces) + len(held))
        + [pl.BlockSpec(memory_space=pltpu.VMEM)] * len(landed),
        out_specs=pl.BlockSpec(memory_space=pltpu.VMEM),
        out_shape=jax.ShapeDtypeStruct((membership.shape[0], query_sum.shape[1]), jnp.float32),
        scratch_shapes=[
            pltpu.VMEM((total, width), pieces[0].dtype),
            pltpu.VMEM((width, across), held[0].dtype),
            pltpu.VMEM((total, across), jnp.float32),
            pltpu.SemaphoreType.DMA((sum(part.shape[0] for part in held),)),
            pltpu.SemaphoreType.DMA((parts, len(pieces))),
        ],
        compiler_params=pltpu.CompilerParams(vmem_limit_bytes=58 * 1024 * 1024),
        cost_estimate=pl.CostEstimate(
            flops=2 * total * width * across,
            bytes_accessed=2 * (total + across) * width,
            transcendentals=0,
        ),
    )(position, mask, membership, query_sum, chosen, *pieces, *held, *landed)


def per_device(
    activations,
    gate_gradient,
    routes,
    sequence_ids,
    input_basis,
    output_basis,
    input_query,
    output_query,
):
    blocks = lax.axis_size("dp")
    group = lax.axis_size("expert")
    halves = group // CORES
    place = lax.axis_index("dp")
    member = lax.axis_index("expert")
    half = member // CORES
    core = member % CORES
    tokens, top = routes.shape
    columns = input_query.shape[2]
    queries = columns // RANK
    count = bits_of(blocks)

    def send(packed, bit):
        return lax.ppermute(packed, "dp", flip(blocks, 1 << bit))

    def own_shard(total):
        shard = total.astype(jnp.bfloat16)
        return shard.reshape(halves, -1, columns)

    def exchange(shard):
        pieces = [shard[0]] + [
            lax.ppermute(shard[d], "expert", flip(group, d * CORES)) for d in range(1, halves)
        ]
        return jnp.concatenate(pieces, axis=1)

    def from_half(part, d):
        return part if d == 0 else lax.ppermute(part, "expert", flip(group, d * CORES))

    def from_core(part):
        return lax.ppermute(part, "expert", flip(group, 1))

    order_first = [(i + 1) % count for i in range(count)]
    order_second = list(range(count))
    position = jnp.stack([place, half]).astype(jnp.int32)
    own = jnp.concatenate([column_exponent(input_query[0]), column_exponent(output_query[0])])

    def joined(keep, landed, exponent):
        total = keep + unpack(landed, exponent)
        middle = total.shape[0] // 2
        return total[:middle], total[middle:]

    send_first, keep_first = fold_partial(
        input_basis[0], input_query[0], own[0:1], position, order_first, halves
    )
    there = [send(own, order_first[0])]
    whole = jnp.maximum(own, there[0])
    there_second = send(own, order_second[0])[1:2]
    send_first, whole = tie(send_first, whole)
    for bit in order_first[1:-1]:
        whole = jnp.maximum(whole, send(whole, bit))
    packed_first = send_first.astype(jnp.float16)
    output_basis, packed_first = tie(output_basis, packed_first)
    landed_first = send(packed_first, order_first[0])

    send_second, keep_second = fold_partial(
        output_basis[0], output_query[0], own[1:2], position, order_second, halves
    )
    send_second, whole = tie(send_second, whole)
    whole = jnp.maximum(whole, send(whole, order_first[-1]))
    packed_second = send_second.astype(jnp.float16)
    activations, routes, packed_second = tie(activations, routes, packed_second)
    landed_second = send(packed_second, order_second[0])

    input_width = activations.shape[1] // halves
    input_parts = [
        lax.dynamic_slice_in_dim(activations, (half ^ d) * input_width, input_width, axis=1)
        for d in range(halves)
    ]
    keep_first, *input_parts = tie(keep_first, *input_parts)
    input_parts = [from_half(part, d) for d, part in enumerate(input_parts)]
    keep_first, send_first = joined(keep_first, landed_first, there[0][0:1])
    packed_first = pack(send_first, whole[0:1] + 1)
    gate_gradient, routes, packed_first = tie(gate_gradient, routes, packed_first)
    landed_first = send(packed_first, order_first[1])

    small = jnp.concatenate([routes.T, sequence_ids], axis=0)
    small = jnp.stack(
        [small] + [lax.ppermute(small, "expert", flip(group, d)) for d in range(1, group)]
    )
    group_routes = small[:, :top].transpose(0, 2, 1).reshape(-1)
    group_sequences = small[:, top]
    gradient = gate_gradient.reshape(tokens * top, -1)
    gradient_width = gradient.shape[1] // halves

    def gradient_part(d, start, size):
        return lax.dynamic_slice(
            gradient, (start, (half ^ d) * gradient_width), (size, gradient_width)
        )

    others = range(1, halves)
    quarter = tokens * top // 4
    early, middle, late = [
        [gradient_part(d, start, size) for d in others]
        for start, size in ((0, quarter), (quarter, quarter), (2 * quarter, 2 * quarter))
    ]
    early = [from_half(part, d) for d, part in zip(others, early)]

    for stage, bit in list(enumerate(order_first))[2:]:
        keep_first, send_first = joined(keep_first, landed_first, whole[0:1] + stage - 1)
        if stage + 1 == count:
            send_first, *input_parts = tie(send_first, *input_parts)
        landed_first = send(pack(send_first, whole[0:1] + stage), bit)
    shard_first = own_shard(keep_first + unpack(landed_first, whole[0:1] + count - 1))
    shard_first, *early = tie(shard_first, *early)
    shard_first, *middle = tie(exchange(shard_first), *middle)
    middle = [from_half(part, d) for d, part in zip(others, middle)]

    keep_second, send_second = joined(keep_second, landed_second, there_second)
    for stage, bit in list(enumerate(order_second))[1:]:
        if stage + 1 == count:
            send_second, shard_first = tie(send_second, shard_first)
        landed_second = send(pack(send_second, whole[1:2] + stage), bit)
        if stage + 1 < count:
            keep_second, send_second = joined(keep_second, landed_second, whole[1:2] + stage)
    shard_second = own_shard(keep_second + unpack(landed_second, whole[1:2] + count - 1))
    shard_second, *middle = tie(shard_second, *middle)
    shard_second, *late = tie(exchange(shard_second), *late)
    late = [from_half(part, d) for d, part in zip(others, late)]

    fold_input = lax.all_gather(shard_first, "dp", axis=0, tiled=True)
    gather_orders = [order_second, order_second[1:] + order_second[:1]]
    held_output = []
    rows = shard_second.shape[0] // len(gather_orders)
    for n, order in enumerate(gather_orders):
        held = shard_second[n * rows : (n + 1) * rows][None]
        for bit in order[:0:-1]:
            held = jnp.concatenate([held, send(held, bit)])
        held_output += [held, send(held, order[0])]

    input_pieces = []
    for part in input_parts:
        input_pieces += [part, from_core(part)]
    own_gradient = gradient_part(0, 0, tokens * top)
    gradient_pieces = [own_gradient, from_core(own_gradient)]
    for pieces in zip(early, middle, late):
        gradient_pieces += pieces
        gradient_pieces += [from_core(piece) for piece in pieces]

    experts = (half ^ jnp.arange(halves, dtype=jnp.int32)) * CORES + core
    mask = (group_routes[None, :, None] == experts[:, None, None]).astype(jnp.float32)
    mask = jnp.broadcast_to(mask, (halves, group_routes.shape[0], columns))
    chosen, sent = input_chosen(input_pieces, fold_input, mask, top)
    landed = [lax.ppermute(sent, "expert", flip(group, d * CORES)) for d in others]

    member_of = jnp.arange(group, dtype=jnp.int32)[:, None] * SEG_DEV
    row_of = jnp.repeat((group_sequences + member_of).reshape(-1), top)
    membership = (
        jnp.arange(group * SEG_DEV, dtype=jnp.int32)[:, None] == row_of[None, :]
    ).astype(jnp.float32)
    column_query = jnp.arange(columns, dtype=jnp.int32) // RANK
    query_sum = (
        column_query[:, None] == jnp.arange(queries, dtype=jnp.int32)[None, :]
    ).astype(jnp.float32)
    partial = partial_scores(
        gradient_pieces,
        held_output,
        gather_orders,
        position,
        mask,
        membership,
        query_sum,
        chosen,
        landed,
    )
    partial = partial.reshape(group, SEG_DEV, queries)
    scores = partial[0]
    for d in range(1, group):
        scores = scores + lax.ppermute(partial[d], "expert", flip(group, d))
    return scores


def solution(mesh):
    return jax.shard_map(
        per_device,
        mesh=mesh,
        in_specs=(
            P(("dp", "expert"), None),
            P(("dp", "expert"), None, None),
            P(("dp", "expert"), None),
            P(("dp", "expert"), None),
            P("expert", None, "dp"),
            P("expert", None, "dp"),
            P("expert", "dp", None),
            P("expert", "dp", None),
        ),
        out_specs=P(("dp", "expert"), None),
        check_vma=False,
    )
```

```python
import functools

import jax
import jax.numpy as jnp
import numpy as np
from jax import lax
from jax.experimental import pallas as pl
from jax.experimental.pallas import tpu as pltpu
from jax.sharding import PartitionSpec as P

RANK = 32
SEG_DEV = 4
CORES = 2
TOP_EXPONENT = 15.0
TAIL = 16


def bits_of(count):
    return (count - 1).bit_length()


def slot_order(order):
    width = len(order)
    return [
        sum(((slot >> (width - 1 - i)) & 1) << bit for i, bit in enumerate(order))
        for slot in range(1 << width)
    ]


def column_exponent(query):
    peak = jnp.max(jnp.abs(query).astype(jnp.float32), axis=0, keepdims=True)
    bound = jnp.maximum(peak * (0.25 * query.shape[0]), 1e-28)
    return jnp.floor(jnp.log2(bound)) + 1.0


def fold_kernel(width, steps, scaled, *refs):
    basis_refs, refs = refs[1 : 1 + 2 * width], refs[1 + 2 * width :]
    query_refs, out_refs, sum_refs, done = refs[:2], refs[2:4], refs[4:6], refs[6]
    step = pl.program_id(0)
    for chunk in range(2):
        query_ref, out_ref, sum_ref = query_refs[chunk], out_refs[chunk], sum_refs[chunk]
        chunk_refs = basis_refs[chunk * width : (chunk + 1) * width]
        rows = chunk_refs[0].shape[0]

        def piece(index):
            here = pl.ds(index * (width * rows), width * rows)
            return pltpu.make_async_copy(
                sum_ref.at[here, :], out_ref.at[here, :], done.at[chunk, index]
            )

        here = pl.ds(steps * width * rows, TAIL)
        tail = pltpu.make_async_copy(
            sum_ref.at[here, :], out_ref.at[here, :], done.at[chunk, steps]
        )
        for index in range(steps):

            @pl.when(step == chunk * steps + index)
            def _():
                exponent = column_exponent(query_ref[...])
                for part, basis_ref in enumerate(chunk_refs):
                    terms = jnp.dot(
                        basis_ref[...], query_ref[...], preferred_element_type=jnp.float32
                    )
                    if scaled:
                        terms = terms * jnp.exp2(TOP_EXPONENT - exponent)
                    sum_ref[pl.ds((index * width + part) * rows, rows), :] = terms
                piece(index).start()
                if index == 0:
                    sum_ref[here, :] = jnp.broadcast_to(exponent, (TAIL, sum_ref.shape[1]))
                    tail.start()

        @pl.when(step == 2 * steps - 1)
        def _():
            for index in range(steps):
                piece(index).wait()
            tail.wait()


def fold_parts(bases, queries, position, orders, halves, upper):
    columns = queries[0].shape[1]
    blocks = 1 << len(orders[0])
    count = blocks * halves
    width = min(4, count // 2)
    steps = count // 2 // width

    def block(chunk, part):
        order, basis = orders[chunk], bases[chunk]

        def index(i, position_ref):
            i = jnp.clip(i - chunk * steps, 0, steps - 1)
            slot = (i * width + part) // halves + (blocks // 2 if upper else 0)
            relative = sum(
                ((slot >> (len(order) - 1 - n)) & 1) << bit for n, bit in enumerate(order)
            )
            here = (i * width + part) % halves ^ position_ref[1]
            return here * blocks + (relative ^ position_ref[0]), 0

        return pl.BlockSpec((basis.shape[0] // count, basis.shape[1]), index)

    out_shape = [
        jax.ShapeDtypeStruct((basis.shape[0] // 2 + TAIL, columns), jnp.float32)
        for basis in bases
    ]
    return pl.pallas_call(
        functools.partial(fold_kernel, width, steps, upper),
        grid_spec=pltpu.PrefetchScalarGridSpec(
            num_scalar_prefetch=1,
            grid=(2 * steps,),
            in_specs=[block(chunk, part) for chunk in range(2) for part in range(width)]
            + [pl.BlockSpec(query.shape, lambda i, p: (0, 0)) for query in queries],
            out_specs=[pl.BlockSpec(memory_space=pl.ANY)] * 2,
            scratch_shapes=[pltpu.VMEM(out.shape, out.dtype) for out in out_shape]
            + [pltpu.SemaphoreType.DMA((2, steps + 1))],
        ),
        out_shape=out_shape,
        compiler_params=pltpu.CompilerParams(vmem_limit_bytes=56 * 1024 * 1024),
        cost_estimate=pl.CostEstimate(flops=1, bytes_accessed=1, transcendentals=0),
    )(position, *([bases[0]] * width), *([bases[1]] * width), *queries)


def pack(total, exponent):
    half = (total.shape[0] - TAIL) // 2
    scaled = total[half:] * jnp.exp2(TOP_EXPONENT - exponent)
    row = lax.broadcasted_iota(jnp.int32, scaled.shape, 0)
    return jnp.where(row < half, scaled, exponent).astype(jnp.float16)


def unpack(packed):
    tail = packed.shape[0] - TAIL
    exponent = packed[tail : tail + 1].astype(jnp.float32)
    return packed.astype(jnp.float32) * jnp.exp2(exponent - TOP_EXPONENT), exponent


def flip(size, mask):
    return [(i, i ^ mask) for i in range(size)]


def tie(*values):
    return lax.optimization_barrier(values)


def column_kernel(halves, position_ref, source_ref, extra_ref, *out_refs):
    width = source_ref.shape[1]
    for d in range(halves):

        @pl.when(pl.program_id(0) == d)
        def _():
            out_refs[d][:, pl.ds(0, width)] = source_ref[...]
            out_refs[d][:, pl.ds(width, extra_ref.shape[1])] = extra_ref[...]


def column_parts(source, extra, position, halves):
    rows, width = source.shape[0], source.shape[1] // halves
    out_shape = (rows, width + extra.shape[1])
    return pl.pallas_call(
        functools.partial(column_kernel, halves),
        grid_spec=pltpu.PrefetchScalarGridSpec(
            num_scalar_prefetch=1,
            grid=(halves,),
            in_specs=[
                pl.BlockSpec((rows, width), lambda j, p: (0, p[1] ^ j)),
                pl.BlockSpec(extra.shape, lambda j, p: (0, 0)),
            ],
            out_specs=[pl.BlockSpec(out_shape, lambda j, p: (0, 0))] * halves,
        ),
        out_shape=[jax.ShapeDtypeStruct(out_shape, source.dtype)] * halves,
        compiler_params=pltpu.CompilerParams(vmem_limit_bytes=56 * 1024 * 1024),
        cost_estimate=pl.CostEstimate(flops=1, bytes_accessed=1, transcendentals=0),
    )(position, source, extra)


def flatten_kernel(halves, cut, position_ref, source_ref, *out_refs):
    step = pl.program_id(0)
    rows = source_ref.shape[0] * source_ref.shape[1]
    width = source_ref.shape[2] // halves
    for d in range(halves):
        start = pl.multiple_of((position_ref[1] ^ d) * width, width)
        part = source_ref[:, :, pl.ds(start, width)].reshape(rows, width)
        if d == 0:
            out_refs[0][...] = part
            continue

        @pl.when(step < cut)
        def _():
            out_refs[2 * d - 1][...] = part

        @pl.when(step >= cut)
        def _():
            out_refs[2 * d][...] = part


def flattened_parts(source, position, halves, cut):
    tokens, top, width = source.shape
    width = width // halves
    block = 16
    steps, rows = tokens // block, block * top

    def out(index):
        return pl.BlockSpec((rows, width), index)

    specs = [out(lambda i, p: (i, 0))]
    shapes = [(tokens * top, width)]
    for _ in range(1, halves):
        specs += [
            out(lambda i, p: (jnp.minimum(i, cut - 1), 0)),
            out(lambda i, p: (jnp.maximum(i - cut, 0), 0)),
        ]
        shapes += [(cut * rows, width), ((steps - cut) * rows, width)]
    own, *others = pl.pallas_call(
        functools.partial(flatten_kernel, halves, cut),
        grid_spec=pltpu.PrefetchScalarGridSpec(
            num_scalar_prefetch=1,
            grid=(steps,),
            in_specs=[pl.BlockSpec((block, top, width * halves), lambda i, p: (i, 0, 0))],
            out_specs=specs,
        ),
        out_shape=[jax.ShapeDtypeStruct(shape, source.dtype) for shape in shapes],
        compiler_params=pltpu.CompilerParams(vmem_limit_bytes=56 * 1024 * 1024),
        cost_estimate=pl.CostEstimate(
            flops=1, bytes_accessed=4 * source.size, transcendentals=0
        ),
    )(position, source)
    return own, others[0::2], others[1::2]


def start_all(copies, done):
    started = []
    for i, (source, target) in enumerate(copies):
        started.append(pltpu.make_async_copy(source, target, done.at[i]))
        started[i].start()
    return started


def mask_kernel(top, position_ref, *refs):
    *extra_refs, mask_ref, member_ref, rows_ref = refs
    tokens, lanes = extra_refs[0].shape
    lane = lax.broadcasted_iota(jnp.int32, (tokens, lanes), 1).astype(jnp.float32)
    for i, extra_ref in enumerate(extra_refs):
        extra = extra_ref[...].astype(jnp.float32)

        def column(k):
            return jnp.broadcast_to(extra[:, k : k + 1], (tokens, lanes))

        member = jnp.where(column(top) + float(i * SEG_DEV) == lane, 1.0, 0.0)
        for k in range(top):
            rows = pl.ds(i * tokens * top + k, tokens, stride=top)
            rows_ref[rows, :] = member
            for d in range(mask_ref.shape[0]):
                expert = ((position_ref[1] ^ d) * CORES + position_ref[2]).astype(jnp.float32)
                mask_ref[d, rows, :] = jnp.where(column(k) == expert, 1.0, 0.0)
    member_ref[...] = rows_ref[...].astype(member_ref.dtype)


def masks(position, pieces, top, halves, lanes):
    tokens = pieces[0].shape[0]
    rows = len(pieces) * tokens * top
    last = pieces[0].shape[1] // lanes - 1
    return pl.pallas_call(
        functools.partial(mask_kernel, top),
        grid=(1,),
        in_specs=[pl.BlockSpec(memory_space=pltpu.SMEM)]
        + [pl.BlockSpec((tokens, lanes), lambda i: (0, last))] * len(pieces),
        out_specs=[
            pl.BlockSpec((halves, rows, lanes), lambda i: (0, 0, 0)),
            pl.BlockSpec((rows, lanes), lambda i: (0, 0)),
        ],
        out_shape=[
            jax.ShapeDtypeStruct((halves, rows, lanes), jnp.float32),
            jax.ShapeDtypeStruct((rows, lanes), jnp.bfloat16),
        ],
        scratch_shapes=[pltpu.VMEM((rows, lanes), jnp.float32)],
        cost_estimate=pl.CostEstimate(flops=1, bytes_accessed=1, transcendentals=0),
    )(position, *pieces)


def input_kernel(top, layouts, count, position_ref, mask_ref, *refs):
    *refs, out_ref, sent_ref, tokens_ref, held_ref, done = refs
    token_refs, fold_refs = refs[:count], refs[count:]
    rows = token_refs[0].shape[0]
    copies = [
        (token_ref.at[:, pl.ds(0, tokens_ref.shape[1])], tokens_ref.at[pl.ds(i * rows, rows), :])
        for i, token_ref in enumerate(token_refs)
    ]
    for fold_ref, (relatives, offset, block) in zip(fold_refs, layouts):
        rows = fold_ref.shape[1]
        for slot, relative in enumerate(relatives):
            start = pl.multiple_of((relative ^ position_ref[0]) * block + offset, 16)
            copies.append((fold_ref.at[slot], held_ref.at[pl.ds(start, rows), :]))
    for copy in start_all(copies, done):
        copy.wait()
    terms = jnp.dot(tokens_ref[...], held_ref[...], preferred_element_type=jnp.float32)
    total = tokens_ref.shape[0]
    columns = out_ref.shape[1]
    for k in range(top):
        rows_of = pl.ds(k, total, stride=top)
        out_ref[rows_of, :] = sum(
            terms[:, d * columns : (d + 1) * columns] * mask_ref[d, rows_of, :]
            for d in range(mask_ref.shape[0])
        )
    sent_ref[...] = out_ref[...].astype(sent_ref.dtype)


def input_chosen(position, pieces, held, orders, mask, top):
    total = sum(piece.shape[0] for piece in pieces)
    columns = mask.shape[2]
    width, across = pieces[0].shape[1] - columns, held[0].shape[2]
    block = sum(part.shape[1] for part in held[0::2])
    layouts, offset = [], 0
    for first, last, order in zip(held[0::2], held[1::2], orders):
        relatives = slot_order(order)
        middle = first.shape[0]
        layouts += [(relatives[:middle], offset, block), (relatives[middle:], offset, block)]
        offset += first.shape[1]
    slots = sum(part.shape[0] for part in held)
    return pl.pallas_call(
        functools.partial(input_kernel, top, layouts, len(pieces)),
        in_specs=[pl.BlockSpec(memory_space=pltpu.SMEM), pl.BlockSpec(memory_space=pltpu.VMEM)]
        + [pl.BlockSpec(memory_space=pl.ANY)] * (len(pieces) + len(held)),
        out_specs=[pl.BlockSpec(memory_space=pltpu.VMEM)] * 2,
        out_shape=[
            jax.ShapeDtypeStruct((total * top, columns), jnp.float32),
            jax.ShapeDtypeStruct((total * top, columns), jnp.bfloat16),
        ],
        scratch_shapes=[
            pltpu.VMEM((total, width), pieces[0].dtype),
            pltpu.VMEM((width, across), held[0].dtype),
            pltpu.SemaphoreType.DMA((len(pieces) + slots,)),
        ],
        compiler_params=pltpu.CompilerParams(vmem_limit_bytes=58 * 1024 * 1024),
        cost_estimate=pl.CostEstimate(flops=1, bytes_accessed=1, transcendentals=0),
    )(position, mask, *pieces, *held)


def spans(counts):
    starts = [sum(counts[:i]) for i in range(len(counts))]
    return list(zip(starts, counts))


def output_terms(position_ref, layouts, aligned, token_refs, fold_refs, buffers):
    tokens_ref, fold_ref, total_ref, folded, done = buffers
    counts = [token_ref.shape[0] for token_ref in token_refs]
    fold_copies, token_copies, row = [], [], 0
    for held_ref, (relatives, part, size) in zip(fold_refs, layouts):
        rows = held_ref.shape[1]
        for slot, relative in enumerate(relatives):
            block = (relative ^ position_ref[0]) * size + part
            target = row if aligned else pl.multiple_of(block * rows, rows)
            fold_copies.append((held_ref.at[slot], fold_ref.at[pl.ds(target, rows), :]))
            if aligned:
                across = pl.ds(row, rows)
                token_copies.append(
                    [
                        (
                            token_ref.at[:, pl.ds(pl.multiple_of(block * rows, rows), rows)],
                            tokens_ref.at[pl.ds(first, count), across],
                        )
                        for token_ref, (first, count) in zip(token_refs, spans(counts))
                    ]
                )
            row += rows
    if not aligned:
        token_copies = [
            [
                (token_ref, tokens_ref.at[pl.ds(first, count), :])
                for token_ref, (first, count) in zip(token_refs, spans(counts))
            ]
        ]
    fold_copies = start_all(fold_copies, folded)
    token_copies = [start_all(copies, done.at[i]) for i, copies in enumerate(token_copies)]
    for copy in fold_copies:
        copy.wait()
    for copies in token_copies:
        for copy in copies:
            copy.wait()
    total_ref[...] = jnp.dot(
        tokens_ref[...], fold_ref[...], preferred_element_type=jnp.float32
    )


def score_kernel(layouts, aligned, count, landed_count, position_ref, *refs):
    member_ref, query_ref, *refs = refs
    first = landed_count is not None
    if first:
        mask_ref, chosen_ref, *refs = refs
        landed_refs, refs = refs[:landed_count], refs[landed_count:]
    else:
        before_ref, weight_in_ref, *refs = refs
    token_refs, refs = refs[:count], refs[count:]
    *fold_refs, out_ref, weight_ref, tokens_ref, fold_ref, total_ref, folded, done, sent = refs
    if not first:
        weight_copy = pltpu.make_async_copy(weight_in_ref, weight_ref, sent)
        weight_copy.start()
    output_terms(
        position_ref,
        layouts,
        aligned,
        token_refs,
        fold_refs,
        (tokens_ref, fold_ref, total_ref, folded, done),
    )
    halves, total, columns = weight_ref.shape
    if first:
        rows = total // halves
        for h in range(halves):
            here = pl.ds(h * rows, rows)
            inputs = chosen_ref[here, :]
            for d, landed_ref in enumerate(landed_refs):
                landed = landed_ref[pl.ds((h ^ (d + 1)) * rows, rows), :]
                inputs = inputs + landed.astype(jnp.float32)
            for d in range(halves):
                weight_ref[d, here, :] = inputs * mask_ref[d, here, :]
    else:
        weight_copy.wait()
    products = sum(
        total_ref[:, d * columns : (d + 1) * columns] * weight_ref[d] for d in range(halves)
    )
    high = products.astype(jnp.bfloat16)
    low = (products - high.astype(jnp.float32)).astype(jnp.bfloat16)
    summed = sum(
        lax.dot_general(
            member_ref[...],
            part,
            (((0,), (0,)), ((), ())),
            preferred_element_type=jnp.float32,
        )
        for part in (high, low)
    )
    scores = jnp.dot(
        summed,
        query_ref[...],
        precision=lax.Precision.HIGHEST,
        preferred_element_type=jnp.float32,
    )
    scores = scores[: out_ref.shape[0]]
    out_ref[...] = scores if first else scores + before_ref[...]


def score_call(position, membership, query_sum, sequences, values, landed, pieces, folds, layouts, aligned):
    first = landed is not None
    total = sum(piece.shape[0] for piece in pieces)
    across = folds[0].shape[2]
    width = sum(fold.shape[0] * fold.shape[1] for fold in folds)
    slots = sum(fold.shape[0] for fold in folds)
    weights = values[0] if first else values[1]
    scores = jax.ShapeDtypeStruct((sequences, query_sum.shape[1]), jnp.float32)
    vmem, anywhere = pl.BlockSpec(memory_space=pltpu.VMEM), pl.BlockSpec(memory_space=pl.ANY)
    weight_scratch = pltpu.VMEM(weights.shape, jnp.float32)
    out = pl.pallas_call(
        functools.partial(
            score_kernel, layouts, aligned, len(pieces), len(landed) if first else None
        ),
        in_specs=[pl.BlockSpec(memory_space=pltpu.SMEM)]
        + [vmem] * 2
        + ([vmem] * (2 + len(landed)) if first else [vmem, anywhere])
        + [anywhere] * (len(pieces) + len(folds)),
        out_specs=[vmem] * 2 if first else vmem,
        out_shape=[scores, jax.ShapeDtypeStruct(weights.shape, jnp.float32)] if first else scores,
        scratch_shapes=([] if first else [weight_scratch])
        + [
            pltpu.VMEM((total, width), pieces[0].dtype),
            pltpu.VMEM((width, across), folds[0].dtype),
            pltpu.VMEM((total, across), jnp.float32),
            pltpu.SemaphoreType.DMA((slots,)),
            pltpu.SemaphoreType.DMA((slots if aligned else 1, len(pieces))),
            pltpu.SemaphoreType.DMA,
        ],
        compiler_params=pltpu.CompilerParams(vmem_limit_bytes=58 * 1024 * 1024),
        cost_estimate=pl.CostEstimate(flops=1, bytes_accessed=1, transcendentals=0),
    )(position, membership, query_sum, *values, *(landed or []), *pieces, *folds)
    return out


def partial_scores(
    pieces, held, orders, position, mask, membership, query_sum, sequences, chosen, landed
):
    halves_of = [[], []]
    for n, order in enumerate(orders):
        relatives = slot_order(order)
        middle = len(relatives) // 2
        for side in range(2):
            chunk = relatives[side * middle : (side + 1) * middle]
            halves_of[side].append((chunk, n, len(orders)))
    firsts, lasts = held[0::2], held[1::2]
    if held[0].shape[1] % 128 != 0:
        scores, _ = score_call(
            position,
            membership,
            query_sum,
            sequences,
            [mask, chosen],
            landed,
            pieces,
            firsts + lasts,
            halves_of[0] + halves_of[1],
            False,
        )
        return scores
    scores, weights = score_call(
        position,
        membership,
        query_sum,
        sequences,
        [mask, chosen],
        landed,
        pieces,
        firsts,
        halves_of[0],
        True,
    )
    return score_call(
        position,
        membership,
        query_sum,
        sequences,
        [scores, weights],
        None,
        pieces,
        lasts,
        halves_of[1],
        True,
    )


def per_device(
    activations,
    gate_gradient,
    routes,
    sequence_ids,
    input_basis,
    output_basis,
    input_query,
    output_query,
):
    blocks = lax.axis_size("dp")
    group = lax.axis_size("expert")
    halves = group // CORES
    place = lax.axis_index("dp")
    member = lax.axis_index("expert")
    half = member // CORES
    core = member % CORES
    tokens, top = routes.shape
    columns = input_query.shape[2]
    queries = columns // RANK
    count = bits_of(blocks)

    def send(packed, bit):
        return lax.ppermute(packed, "dp", flip(blocks, 1 << bit))

    def joined(keep, landed, exponent):
        values, there = unpack(landed)
        total = keep + values
        exponent = jnp.maximum(exponent, there) + 1
        return total, exponent, total[: (total.shape[0] - TAIL) // 2 + TAIL]

    def own_shard(keep, landed):
        total = (keep + unpack(landed)[0]).astype(jnp.bfloat16)
        return total[: total.shape[0] - TAIL].reshape(halves, -1, columns)

    def exchange(shard):
        pieces = [shard[0]] + [
            lax.ppermute(shard[d], "expert", flip(group, d * CORES)) for d in range(1, halves)
        ]
        return jnp.concatenate(pieces, axis=1)

    def from_half(part, d):
        return part if d == 0 else lax.ppermute(part, "expert", flip(group, d * CORES))

    def from_core(part):
        return lax.ppermute(part, "expert", flip(group, 1))

    order_first = [(i + 1) % count for i in range(count)]
    order_second = list(range(count))
    position = jnp.stack([place, half, core]).astype(jnp.int32)

    def parts(bases, upper):
        queries = (input_query[0], output_query[0])
        return fold_parts(bases, queries, position, (order_first, order_second), halves, upper)

    bases = input_basis[0], output_basis[0]
    packed_first, packed_second = [part.astype(jnp.float16) for part in parts(bases, True)]
    *bases, packed_first, packed_second = tie(*bases, packed_first, packed_second)
    landed_first = send(packed_first, order_first[0])
    landed_second = send(packed_second, order_second[0])
    exponent_first = column_exponent(input_query[0])
    exponent_second = column_exponent(output_query[0])

    others = range(1, halves)
    gather_orders = [order_second, order_second[1:] + order_second[:1]]
    keep_first, keep_second = parts(bases, False)
    activations, keep_first = tie(activations, keep_first)
    extra = jnp.concatenate([routes, sequence_ids.T], axis=1).astype(jnp.bfloat16)
    extra = jnp.pad(extra, ((0, 0), (0, columns - extra.shape[1])))
    input_parts = list(column_parts(activations, extra, position, halves))
    landed_first, *input_parts = tie(landed_first, *input_parts)
    input_parts = [from_half(part, d) for d, part in enumerate(input_parts)]

    total, exponent_first, keep_first = joined(keep_first, landed_first, exponent_first)
    landed_first = send(pack(total, exponent_first), order_first[1])
    total, exponent_second, keep_second = joined(keep_second, landed_second, exponent_second)
    packed_second = pack(total, exponent_second)
    gate_gradient, packed_second = tie(gate_gradient, packed_second)
    landed_second = send(packed_second, order_second[1])
    own_gradient, early, late = flattened_parts(
        gate_gradient, position, halves, tokens // 16 // 4
    )
    landed_first, own_gradient = tie(landed_first, own_gradient)

    for bit in order_first[2:]:
        total, exponent_first, keep_first = joined(keep_first, landed_first, exponent_first)
        landed_first = send(pack(total, exponent_first), bit)
    for bit in order_second[2:]:
        total, exponent_second, keep_second = joined(
            keep_second, landed_second, exponent_second
        )
        packed_second = pack(total, exponent_second)
        packed_second, landed_first = tie(packed_second, landed_first)
        landed_second = send(packed_second, bit)
    own_half, *input_parts = input_parts
    shard_first, *input_parts = tie(own_shard(keep_first, landed_first), *input_parts)
    input_pieces = [own_half, from_core(own_half)]
    for part in input_parts:
        input_pieces += [part, from_core(part)]
    swapped_gradient = from_core(own_gradient)
    mask, membership = masks(position, input_pieces, top, halves, columns)
    query_sum = jnp.asarray(
        np.arange(columns)[:, None] // RANK == np.arange(queries)[None, :], jnp.float32
    )

    def split(shard):
        cut = (shard.shape[0] // len(gather_orders) + 15) // 16 * 16
        return [shard[:cut][None], shard[cut:][None]]

    def stage_of(held, stage):
        return [send(part, bits[stage]) for part, bits in zip(held, gather_orders)]

    def both(held, landed):
        return [jnp.concatenate(pair) for pair in zip(held, landed)]

    shard_first, *early = tie(exchange(shard_first), *early)
    early = [from_half(part, d) for d, part in zip(others, early)]
    held_first = shard_first[None]
    landed_first = send(held_first, order_second[-1])
    landed_second, mask, membership, swapped_gradient = tie(
        landed_second, mask, membership, swapped_gradient
    )
    shard_second = own_shard(keep_second, landed_second)
    shard_second, landed_first, *early = tie(shard_second, landed_first, *early)
    swapped_early = [from_core(part) for part in early]
    shard_second, *late = tie(exchange(shard_second), *late)
    held_first = jnp.concatenate([held_first, landed_first])
    late = [from_half(part, d) for d, part in zip(others, late)]
    held_second = split(shard_second)
    for stage in range(2, count):
        landed_first = send(held_first, order_second[-stage])
        landed = stage_of(held_second, 1 - stage)
        landed_first, *landed = tie(landed_first, *landed, *swapped_early)
        landed, swapped_early = landed[:2], landed[2:]
        held_first = jnp.concatenate([held_first, landed_first])
        held_second = both(held_second, landed)
    last_first = send(held_first, order_second[0])
    last_first, *landed = tie(last_first, *stage_of(held_second, 1 - count))
    held_second = both(held_second, landed)
    last_second = stage_of(held_second, 0)
    held_output = [held_second[0], last_second[0], held_second[1], last_second[1]]

    chosen, sent = input_chosen(
        position, input_pieces, [held_first, last_first], [order_second], mask, top
    )
    sent, *late = tie(sent, *late)
    landed = [lax.ppermute(sent, "expert", flip(group, d * CORES)) for d in others]

    gradient_pieces = [own_gradient, swapped_gradient]
    for first_part, last_part, swapped_part in zip(early, late, swapped_early):
        gradient_pieces += [first_part, last_part, swapped_part, from_core(last_part)]

    partial = partial_scores(
        gradient_pieces,
        held_output,
        gather_orders,
        position,
        mask,
        membership,
        query_sum,
        group * SEG_DEV,
        chosen,
        landed,
    )
    partial = partial.reshape(group, SEG_DEV, queries)
    scores = partial[0]
    for d in range(1, group):
        scores = scores + lax.ppermute(partial[d], "expert", flip(group, d))
    return scores


def solution(mesh):
    return jax.shard_map(
        per_device,
        mesh=mesh,
        in_specs=(
            P(("dp", "expert"), None),
            P(("dp", "expert"), None, None),
            P(("dp", "expert"), None),
            P(("dp", "expert"), None),
            P("expert", None, "dp"),
            P("expert", None, "dp"),
            P("expert", "dp", None),
            P("expert", "dp", None),
        ),
        out_specs=P(("dp", "expert"), None),
        check_vma=False,
    )
```

```python
import functools

import jax
import jax.numpy as jnp
import numpy as np
from jax import lax
from jax.experimental import pallas as pl
from jax.experimental.pallas import tpu as pltpu
from jax.sharding import PartitionSpec as P

RANK = 32
SEG_DEV = 4
CORES = 2
TOP_EXPONENT = 15.0
TAIL = 16


def bits_of(count):
    return (count - 1).bit_length()


def slot_order(order):
    width = len(order)
    return [
        sum(((slot >> (width - 1 - i)) & 1) << bit for i, bit in enumerate(order))
        for slot in range(1 << width)
    ]


def column_exponent(query):
    peak = jnp.max(jnp.abs(query).astype(jnp.float32), axis=0, keepdims=True)
    bound = jnp.maximum(peak * (0.25 * query.shape[0]), 1e-28)
    return jnp.floor(jnp.log2(bound)) + 1.0


def fold_kernel(width, steps, scaled, *refs):
    basis_refs, refs = refs[1 : 1 + 2 * width], refs[1 + 2 * width :]
    query_refs, out_refs, sum_refs, done = refs[:2], refs[2:4], refs[4:6], refs[6]
    step = pl.program_id(0)
    for chunk in range(2):
        query_ref, out_ref, sum_ref = query_refs[chunk], out_refs[chunk], sum_refs[chunk]
        chunk_refs = basis_refs[chunk * width : (chunk + 1) * width]
        rows = chunk_refs[0].shape[0]

        def piece(index):
            here = pl.ds(index * (width * rows), width * rows)
            return pltpu.make_async_copy(
                sum_ref.at[here, :], out_ref.at[here, :], done.at[chunk, index]
            )

        here = pl.ds(steps * width * rows, TAIL)
        tail = pltpu.make_async_copy(
            sum_ref.at[here, :], out_ref.at[here, :], done.at[chunk, steps]
        )
        for index in range(steps):

            @pl.when(step == chunk * steps + index)
            def _():
                exponent = column_exponent(query_ref[...])
                for part, basis_ref in enumerate(chunk_refs):
                    terms = jnp.dot(
                        basis_ref[...], query_ref[...], preferred_element_type=jnp.float32
                    )
                    if scaled:
                        terms = terms * jnp.exp2(TOP_EXPONENT - exponent)
                    sum_ref[pl.ds((index * width + part) * rows, rows), :] = terms
                piece(index).start()
                if index == 0:
                    sum_ref[here, :] = jnp.broadcast_to(exponent, (TAIL, sum_ref.shape[1]))
                    tail.start()

        @pl.when(step == 2 * steps - 1)
        def _():
            for index in range(steps):
                piece(index).wait()
            tail.wait()


def fold_parts(bases, queries, position, orders, halves, upper):
    columns = queries[0].shape[1]
    blocks = 1 << len(orders[0])
    count = blocks * halves
    width = min(4, count // 2)
    steps = count // 2 // width

    def block(chunk, part):
        order, basis = orders[chunk], bases[chunk]

        def index(i, position_ref):
            i = jnp.clip(i - chunk * steps, 0, steps - 1)
            slot = (i * width + part) // halves + (blocks // 2 if upper else 0)
            relative = sum(
                ((slot >> (len(order) - 1 - n)) & 1) << bit for n, bit in enumerate(order)
            )
            here = (i * width + part) % halves ^ position_ref[1]
            return here * blocks + (relative ^ position_ref[0]), 0

        return pl.BlockSpec((basis.shape[0] // count, basis.shape[1]), index)

    out_shape = [
        jax.ShapeDtypeStruct((basis.shape[0] // 2 + TAIL, columns), jnp.float32)
        for basis in bases
    ]
    return pl.pallas_call(
        functools.partial(fold_kernel, width, steps, upper),
        grid_spec=pltpu.PrefetchScalarGridSpec(
            num_scalar_prefetch=1,
            grid=(2 * steps,),
            in_specs=[block(chunk, part) for chunk in range(2) for part in range(width)]
            + [pl.BlockSpec(query.shape, lambda i, p: (0, 0)) for query in queries],
            out_specs=[pl.BlockSpec(memory_space=pl.ANY)] * 2,
            scratch_shapes=[pltpu.VMEM(out.shape, out.dtype) for out in out_shape]
            + [pltpu.SemaphoreType.DMA((2, steps + 1))],
        ),
        out_shape=out_shape,
        compiler_params=pltpu.CompilerParams(vmem_limit_bytes=56 * 1024 * 1024),
        cost_estimate=pl.CostEstimate(flops=1, bytes_accessed=1, transcendentals=0),
    )(position, *([bases[0]] * width), *([bases[1]] * width), *queries)


def pack(keep, landed, there, exponent):
    half = (keep.shape[0] - TAIL) // 2
    values = landed[half:].astype(jnp.float32) * jnp.exp2(there - TOP_EXPONENT)
    scaled = (keep[half:] + values) * jnp.exp2(TOP_EXPONENT - exponent)
    row = lax.broadcasted_iota(jnp.int32, scaled.shape, 0)
    return jnp.where(row < half, scaled, exponent).astype(jnp.float16)


def flip(size, mask):
    return [(i, i ^ mask) for i in range(size)]


def tie(*values):
    return lax.optimization_barrier(values)


def column_kernel(halves, position_ref, source_ref, extra_ref, *out_refs):
    width = source_ref.shape[1]
    for d in range(halves):

        @pl.when(pl.program_id(0) == d)
        def _():
            out_refs[d][:, pl.ds(0, width)] = source_ref[...]
            out_refs[d][:, pl.ds(width, extra_ref.shape[1])] = extra_ref[...]


def column_parts(source, extra, position, halves):
    rows, width = source.shape[0], source.shape[1] // halves
    out_shape = (rows, width + extra.shape[1])
    return pl.pallas_call(
        functools.partial(column_kernel, halves),
        grid_spec=pltpu.PrefetchScalarGridSpec(
            num_scalar_prefetch=1,
            grid=(halves,),
            in_specs=[
                pl.BlockSpec((rows, width), lambda j, p: (0, p[1] ^ j)),
                pl.BlockSpec(extra.shape, lambda j, p: (0, 0)),
            ],
            out_specs=[pl.BlockSpec(out_shape, lambda j, p: (0, 0))] * halves,
        ),
        out_shape=[jax.ShapeDtypeStruct(out_shape, source.dtype)] * halves,
        compiler_params=pltpu.CompilerParams(vmem_limit_bytes=56 * 1024 * 1024),
        cost_estimate=pl.CostEstimate(flops=1, bytes_accessed=1, transcendentals=0),
    )(position, source, extra)


def flatten_kernel(halves, cuts, position_ref, source_ref, *out_refs):
    step = pl.program_id(0)
    rows = source_ref.shape[0] * source_ref.shape[1]
    width = source_ref.shape[2] // halves
    for d in range(halves):
        start = pl.multiple_of((position_ref[1] ^ d) * width, width)
        part = source_ref[:, :, pl.ds(start, width)].reshape(rows, width)
        if d == 0:
            out_refs[0][...] = part
            continue
        for n in range(len(cuts) - 1):

            @pl.when((step >= cuts[n]) & (step < cuts[n + 1]))
            def _():
                out_refs[1 + n * (halves - 1) + d - 1][...] = part


def flattened_parts(source, position, halves, sizes):
    tokens, top, width = source.shape
    width = width // halves
    block = 16
    steps, rows = tokens // block, block * top
    cuts = [sum(sizes[:n]) for n in range(len(sizes) + 1)] + [steps]

    def out(first, last):
        return pl.BlockSpec((rows, width), lambda i, p: (jnp.clip(i, first, last - 1) - first, 0))

    specs, shapes = [out(0, steps)], [(tokens * top, width)]
    for first, last in zip(cuts, cuts[1:]):
        specs += [out(first, last)] * (halves - 1)
        shapes += [((last - first) * rows, width)] * (halves - 1)
    own, *away = pl.pallas_call(
        functools.partial(flatten_kernel, halves, cuts),
        grid_spec=pltpu.PrefetchScalarGridSpec(
            num_scalar_prefetch=1,
            grid=(steps,),
            in_specs=[pl.BlockSpec((block, top, width * halves), lambda i, p: (i, 0, 0))],
            out_specs=specs,
        ),
        out_shape=[jax.ShapeDtypeStruct(shape, source.dtype) for shape in shapes],
        compiler_params=pltpu.CompilerParams(vmem_limit_bytes=56 * 1024 * 1024),
        cost_estimate=pl.CostEstimate(
            flops=1, bytes_accessed=4 * source.size, transcendentals=0
        ),
    )(position, source)
    return own, *[away[n : n + halves - 1] for n in range(0, len(away), halves - 1)]


def start_all(copies, done):
    started = []
    for i, (source, target) in enumerate(copies):
        started.append(pltpu.make_async_copy(source, target, done.at[i]))
        started[i].start()
    return started


def mask_kernel(top, position_ref, *refs):
    *extra_refs, mask_ref, small_mask_ref, member_ref, rows_ref = refs
    tokens, lanes = extra_refs[0].shape
    lane = lax.broadcasted_iota(jnp.int32, (tokens, lanes), 1).astype(jnp.float32)
    for i, extra_ref in enumerate(extra_refs):
        extra = extra_ref[...].astype(jnp.float32)

        def column(k):
            return jnp.broadcast_to(extra[:, k : k + 1], (tokens, lanes))

        member = jnp.where(column(top) + float(i * SEG_DEV) == lane, 1.0, 0.0)
        for k in range(top):
            rows = pl.ds(i * tokens * top + k, tokens, stride=top)
            rows_ref[rows, :] = member
            for d in range(mask_ref.shape[0]):
                expert = ((position_ref[1] ^ d) * CORES + position_ref[2]).astype(jnp.float32)
                mask_ref[d, rows, :] = jnp.where(column(k) == expert, 1.0, 0.0)
    member_ref[...] = rows_ref[...].astype(member_ref.dtype)
    small_mask_ref[...] = mask_ref[...].astype(small_mask_ref.dtype)


def masks(position, pieces, top, halves, lanes):
    tokens = pieces[0].shape[0]
    rows = len(pieces) * tokens * top
    last = pieces[0].shape[1] // lanes - 1
    return pl.pallas_call(
        functools.partial(mask_kernel, top),
        grid=(1,),
        in_specs=[pl.BlockSpec(memory_space=pltpu.SMEM)]
        + [pl.BlockSpec((tokens, lanes), lambda i: (0, last))] * len(pieces),
        out_specs=[
            pl.BlockSpec((halves, rows, lanes), lambda i: (0, 0, 0)),
            pl.BlockSpec((halves, rows, lanes), lambda i: (0, 0, 0)),
            pl.BlockSpec((rows, lanes), lambda i: (0, 0)),
        ],
        out_shape=[
            jax.ShapeDtypeStruct((halves, rows, lanes), jnp.float32),
            jax.ShapeDtypeStruct((halves, rows, lanes), jnp.bfloat16),
            jax.ShapeDtypeStruct((rows, lanes), jnp.bfloat16),
        ],
        scratch_shapes=[pltpu.VMEM((rows, lanes), jnp.float32)],
        cost_estimate=pl.CostEstimate(flops=1, bytes_accessed=1, transcendentals=0),
    )(position, *pieces)


def input_kernel(top, layouts, count, position_ref, mask_ref, *refs):
    *refs, out_ref, sent_ref, tokens_ref, held_ref, done = refs
    token_refs, fold_refs = refs[:count], refs[count:]
    rows = token_refs[0].shape[0]
    copies = [
        (token_ref.at[:, pl.ds(0, tokens_ref.shape[1])], tokens_ref.at[pl.ds(i * rows, rows), :])
        for i, token_ref in enumerate(token_refs)
    ]
    for fold_ref, (relatives, offset, block) in zip(fold_refs, layouts):
        rows = fold_ref.shape[1]
        for slot, relative in enumerate(relatives):
            start = pl.multiple_of((relative ^ position_ref[0]) * block + offset, 16)
            copies.append((fold_ref.at[slot], held_ref.at[pl.ds(start, rows), :]))
    for copy in start_all(copies, done):
        copy.wait()
    terms = jnp.dot(tokens_ref[...], held_ref[...], preferred_element_type=jnp.float32)
    total = tokens_ref.shape[0]
    columns = out_ref.shape[1]
    for k in range(top):
        rows_of = pl.ds(k, total, stride=top)
        out_ref[rows_of, :] = sum(
            terms[:, d * columns : (d + 1) * columns] * mask_ref[d, rows_of, :]
            for d in range(mask_ref.shape[0])
        )
    sent_ref[...] = out_ref[...].astype(sent_ref.dtype)


def input_chosen(position, pieces, held, orders, mask, top):
    total = sum(piece.shape[0] for piece in pieces)
    columns = mask.shape[2]
    width, across = pieces[0].shape[1] - columns, held[0].shape[2]
    block = sum(part.shape[1] for part in held[0::2])
    layouts, offset = [], 0
    for first, last, order in zip(held[0::2], held[1::2], orders):
        relatives = slot_order(order)
        middle = first.shape[0]
        layouts += [(relatives[:middle], offset, block), (relatives[middle:], offset, block)]
        offset += first.shape[1]
    slots = sum(part.shape[0] for part in held)
    return pl.pallas_call(
        functools.partial(input_kernel, top, layouts, len(pieces)),
        in_specs=[pl.BlockSpec(memory_space=pltpu.SMEM), pl.BlockSpec(memory_space=pltpu.VMEM)]
        + [pl.BlockSpec(memory_space=pl.ANY)] * (len(pieces) + len(held)),
        out_specs=[pl.BlockSpec(memory_space=pltpu.VMEM)] * 2,
        out_shape=[
            jax.ShapeDtypeStruct((total * top, columns), jnp.float32),
            jax.ShapeDtypeStruct((total * top, columns), jnp.bfloat16),
        ],
        scratch_shapes=[
            pltpu.VMEM((total, width), pieces[0].dtype),
            pltpu.VMEM((width, across), held[0].dtype),
            pltpu.SemaphoreType.DMA((len(pieces) + slots,)),
        ],
        compiler_params=pltpu.CompilerParams(vmem_limit_bytes=58 * 1024 * 1024),
        cost_estimate=pl.CostEstimate(flops=1, bytes_accessed=1, transcendentals=0),
    )(position, mask, *pieces, *held)


def spans(counts):
    starts = [sum(counts[:i]) for i in range(len(counts))]
    return list(zip(starts, counts))


def output_terms(position_ref, layouts, aligned, token_refs, fold_refs, buffers):
    tokens_ref, fold_ref, total_ref, folded, done = buffers
    counts = [token_ref.shape[0] for token_ref in token_refs]
    fold_copies, token_copies, row = [], [], 0
    for held_ref, (relatives, part, size) in zip(fold_refs, layouts):
        rows = held_ref.shape[1]
        for slot, relative in enumerate(relatives):
            block = (relative ^ position_ref[0]) * size + part
            target = row if aligned else pl.multiple_of(block * rows, rows)
            fold_copies.append((held_ref.at[slot], fold_ref.at[pl.ds(target, rows), :]))
            if aligned:
                across = pl.ds(row, rows)
                token_copies.append(
                    [
                        (
                            token_ref.at[:, pl.ds(pl.multiple_of(block * rows, rows), rows)],
                            tokens_ref.at[pl.ds(first, count), across],
                        )
                        for token_ref, (first, count) in zip(token_refs, spans(counts))
                    ]
                )
            row += rows
    if not aligned:
        token_copies = [
            [
                (token_ref, tokens_ref.at[pl.ds(first, count), :])
                for token_ref, (first, count) in zip(token_refs, spans(counts))
            ]
        ]
    fold_copies = start_all(fold_copies, folded)
    token_copies = [start_all(copies, done.at[i]) for i, copies in enumerate(token_copies)]
    for copy in fold_copies:
        copy.wait()
    for copies in token_copies:
        for copy in copies:
            copy.wait()
    total_ref[...] = jnp.dot(
        tokens_ref[...], fold_ref[...], preferred_element_type=jnp.float32
    )


def first_kernel(layouts, count, position_ref, *refs):
    token_refs, refs = refs[:count], refs[count:]
    *fold_refs, total_ref, tokens_ref, fold_ref, folded, done = refs
    buffers = tokens_ref, fold_ref, total_ref, folded, done
    output_terms(position_ref, layouts, True, token_refs, fold_refs, buffers)


def last_kernel(layouts, aligned, count, extra_count, group, position_ref, *refs):
    query_ref, *refs = refs
    extra_refs, refs = refs[:extra_count], refs[extra_count:]
    token_refs, refs = refs[:count], refs[count:]
    held_refs, refs = refs[-extra_count:], refs[:-extra_count]
    fold_refs, refs = refs[: len(layouts)], refs[len(layouts) :]
    out_refs, (tokens_ref, fold_ref, total_ref, folded, done, extra_done) = refs[:group], refs[group:]
    extra_copies = start_all(list(zip(extra_refs, held_refs)), extra_done)
    buffers = tokens_ref, fold_ref, total_ref, folded, done
    output_terms(position_ref, layouts, aligned, token_refs, fold_refs, buffers)
    for copy in extra_copies:
        copy.wait()
    mask_ref, member_ref, chosen_ref, *refs = held_refs
    halves = mask_ref.shape[0]
    landed_refs, before_refs = refs[: halves - 1], refs[halves - 1 :]
    columns = chosen_ref.shape[1]
    rows = chosen_ref.shape[0] // halves
    summed = 0.0
    for h in range(halves):
        here = pl.ds(h * rows, rows)
        inputs = chosen_ref[here, :]
        for d, landed_ref in enumerate(landed_refs):
            landed = landed_ref[pl.ds((h ^ (d + 1)) * rows, rows), :]
            inputs = inputs + landed.astype(jnp.float32)
        total = total_ref[here, :]
        for before_ref in before_refs:
            total = total + before_ref[here, :]
        products = inputs * sum(
            total[:, d * columns : (d + 1) * columns] * mask_ref[d, here, :].astype(jnp.float32)
            for d in range(halves)
        )
        high = products.astype(jnp.bfloat16)
        low = (products - high.astype(jnp.float32)).astype(jnp.bfloat16)
        for part in (high, low):
            summed = summed + lax.dot_general(
                member_ref[here, :],
                part,
                (((0,), (0,)), ((), ())),
                preferred_element_type=jnp.float32,
            )
    scores = jnp.dot(
        summed,
        query_ref[...],
        precision=lax.Precision.HIGHEST,
        preferred_element_type=jnp.float32,
    )
    for i, out_ref in enumerate(out_refs):
        out_ref[...] = scores[i * SEG_DEV : (i + 1) * SEG_DEV]


def score_call(position, query_sum, extras, group, pieces, folds, layouts, aligned):
    total = sum(piece.shape[0] for piece in pieces)
    across = folds[0].shape[2]
    width = sum(fold.shape[0] * fold.shape[1] for fold in folds)
    slots = sum(fold.shape[0] for fold in folds)
    vmem, anywhere = pl.BlockSpec(memory_space=pltpu.VMEM), pl.BlockSpec(memory_space=pl.ANY)
    smem = pl.BlockSpec(memory_space=pltpu.SMEM)
    totals = jax.ShapeDtypeStruct((total, across), jnp.float32)
    semaphores = [
        pltpu.SemaphoreType.DMA((slots,)),
        pltpu.SemaphoreType.DMA((slots if aligned else 1, len(pieces))),
    ]
    buffers = [
        pltpu.VMEM((total, width), pieces[0].dtype),
        pltpu.VMEM((width, across), folds[0].dtype),
    ]
    options = dict(
        compiler_params=pltpu.CompilerParams(vmem_limit_bytes=58 * 1024 * 1024),
        cost_estimate=pl.CostEstimate(
            flops=1,
            bytes_accessed=1 if extras else 2 * (total + across) * width,
            transcendentals=0,
        ),
    )
    if not extras:
        return pl.pallas_call(
            functools.partial(first_kernel, layouts, len(pieces)),
            in_specs=[smem] + [anywhere] * (len(pieces) + len(folds)),
            out_specs=vmem,
            out_shape=totals,
            scratch_shapes=buffers + semaphores,
            **options,
        )(position, *pieces, *folds)
    scores = jax.ShapeDtypeStruct((SEG_DEV, query_sum.shape[1]), jnp.float32)
    return pl.pallas_call(
        functools.partial(last_kernel, layouts, aligned, len(pieces), len(extras), group),
        in_specs=[smem, vmem] + [anywhere] * (len(extras) + len(pieces) + len(folds)),
        out_specs=[vmem] * group,
        out_shape=[scores] * group,
        scratch_shapes=buffers
        + [pltpu.VMEM(totals.shape, jnp.float32)]
        + semaphores
        + [pltpu.SemaphoreType.DMA((len(extras),))]
        + [pltpu.VMEM(extra.shape, extra.dtype) for extra in extras],
        **options,
    )(position, query_sum, *extras, *pieces, *folds)


def output_layouts(orders):
    sides = [[], []]
    for n, order in enumerate(orders):
        relatives = slot_order(order)
        middle = len(relatives) // 2
        sides[0].append((relatives[:middle], n, len(orders)))
        sides[1].append((relatives[middle:], n, len(orders)))
    return sides


def per_device(
    activations,
    gate_gradient,
    routes,
    sequence_ids,
    input_basis,
    output_basis,
    input_query,
    output_query,
):
    blocks = lax.axis_size("dp")
    group = lax.axis_size("expert")
    halves = group // CORES
    place = lax.axis_index("dp")
    member = lax.axis_index("expert")
    half = member // CORES
    core = member % CORES
    tokens, top = routes.shape
    columns = input_query.shape[2]
    queries = columns // RANK
    count = bits_of(blocks)

    def send(packed, bit):
        return lax.ppermute(packed, "dp", flip(blocks, 1 << bit))

    def joined(keep, landed, exponent):
        half = (keep.shape[0] - TAIL) // 2
        there = landed[2 * half : 2 * half + 1].astype(jnp.float32)
        exponent = jnp.maximum(exponent, there) + 1
        packed = pack(keep, landed, there, exponent)
        here = slice(0, half + TAIL)
        values = landed[here].astype(jnp.float32) * jnp.exp2(there - TOP_EXPONENT)
        return packed, exponent, keep[here] + values

    def own_shard(keep, landed):
        rows = keep.shape[0] - TAIL
        there = landed[rows : rows + 1].astype(jnp.float32)
        values = landed[:rows].astype(jnp.float32) * jnp.exp2(there - TOP_EXPONENT)
        return (keep[:rows] + values).astype(jnp.bfloat16).reshape(halves, -1, columns)

    def exchange(shard):
        pieces = [shard[0]] + [
            lax.ppermute(shard[d], "expert", flip(group, d * CORES)) for d in range(1, halves)
        ]
        return jnp.concatenate(pieces, axis=1)

    def from_half(part, d):
        return part if d == 0 else lax.ppermute(part, "expert", flip(group, d * CORES))

    def from_core(part):
        return lax.ppermute(part, "expert", flip(group, 1))

    order_first = [(i + 1) % count for i in range(count)]
    order_second = list(range(count))
    position = jnp.stack([place, half, core]).astype(jnp.int32)

    def parts(bases, upper):
        queries = (input_query[0], output_query[0])
        return fold_parts(bases, queries, position, (order_first, order_second), halves, upper)

    bases = input_basis[0], output_basis[0]
    packed_first, packed_second = [part.astype(jnp.float16) for part in parts(bases, True)]
    *bases, packed_first, packed_second = tie(*bases, packed_first, packed_second)
    landed_first = send(packed_first, order_first[0])
    landed_second = send(packed_second, order_second[0])
    exponent_first = column_exponent(input_query[0])
    exponent_second = column_exponent(output_query[0])

    others = range(1, halves)
    gather_orders = [order_second, order_second[1:] + order_second[:1]]
    keep_first, keep_second = parts(bases, False)
    activations, keep_first = tie(activations, keep_first)
    extra = jnp.concatenate([routes, sequence_ids.T], axis=1).astype(jnp.bfloat16)
    extra = jnp.pad(extra, ((0, 0), (0, columns - extra.shape[1])))
    input_parts = list(column_parts(activations, extra, position, halves))
    landed_first, *input_parts = tie(landed_first, *input_parts)
    input_parts = [from_half(part, d) for d, part in enumerate(input_parts)]

    packed_first, exponent_first, keep_first = joined(keep_first, landed_first, exponent_first)
    landed_first = send(packed_first, order_first[1])
    packed_second, exponent_second, keep_second = joined(
        keep_second, landed_second, exponent_second
    )
    gate_gradient, packed_second = tie(gate_gradient, packed_second)
    landed_second = send(packed_second, order_second[1])
    own_gradient, *away = flattened_parts(gate_gradient, position, halves, (2,))
    landed_first, own_gradient = tie(landed_first, own_gradient)

    for bit in order_first[2:]:
        packed_first, exponent_first, keep_first = joined(
            keep_first, landed_first, exponent_first
        )
        landed_first = send(packed_first, bit)
    for bit in order_second[2:]:
        packed_second, exponent_second, keep_second = joined(
            keep_second, landed_second, exponent_second
        )
        packed_second, landed_first = tie(packed_second, landed_first)
        landed_second = send(packed_second, bit)
    own_half, *input_parts = input_parts
    shard_first, *input_parts = tie(own_shard(keep_first, landed_first), *input_parts)
    input_pieces = [own_half, from_core(own_half)]
    for part in input_parts:
        input_pieces += [part, from_core(part)]
    swapped_gradient = from_core(own_gradient)
    mask, small_mask, membership = masks(position, input_pieces, top, halves, columns)
    query_sum = jnp.asarray(
        np.arange(columns)[:, None] // RANK == np.arange(queries)[None, :], jnp.float32
    )

    def split(shard):
        cut = (shard.shape[0] // len(gather_orders) + 15) // 16 * 16
        return [shard[:cut][None], shard[cut:][None]]

    def stage_of(held, stage):
        return [send(part, bits[stage]) for part, bits in zip(held, gather_orders)]

    def both(held, landed):
        return [jnp.concatenate(pair) for pair in zip(held, landed)]

    shard_first, *away[0] = tie(exchange(shard_first), *away[0])
    away[0] = [from_half(part, d) for d, part in zip(others, away[0])]
    held_first = shard_first[None]
    landed_first = send(held_first, order_second[-1])
    landed_second, mask, small_mask, membership, swapped_gradient = tie(
        landed_second, mask, small_mask, membership, swapped_gradient
    )
    shard_second = own_shard(keep_second, landed_second)
    shard_second, landed_first, *away[0] = tie(shard_second, landed_first, *away[0])
    swapped = [[from_core(part) for part in away[0]]]
    shard_second, *away[1] = tie(exchange(shard_second), *away[1])
    held_first = jnp.concatenate([held_first, landed_first])
    away[1] = [from_half(part, d) for d, part in zip(others, away[1])]
    held_second = split(shard_second)
    for stage in range(2, count):
        landed_first = send(held_first, order_second[-stage])
        landed = stage_of(held_second, 1 - stage)
        landed_first, *landed = tie(landed_first, *landed, *swapped[0])
        landed, swapped[0] = landed[:2], landed[2:]
        held_first = jnp.concatenate([held_first, landed_first])
        held_second = both(held_second, landed)
    last_first = send(held_first, order_second[0])
    last_first, *landed = tie(last_first, *stage_of(held_second, 1 - count))
    held_second = both(held_second, landed)
    last_second = stage_of(held_second, 0)
    last_first, *away[1] = tie(last_first, *away[1])
    swapped.append([from_core(part) for part in away[1]])

    pieces = [own_gradient, swapped_gradient]
    for d in range(halves - 1):
        pieces += [part[d] for part in away] + [part[d] for part in swapped]
    layouts = output_layouts(gather_orders)
    aligned = held_second[0].shape[1] % 128 == 0
    chosen, sent = input_chosen(
        position, input_pieces, [held_first, last_first], [order_second], mask, top
    )
    before = []
    if aligned:
        sent, *held_second = tie(sent, *held_second)
        before = [
            score_call(
                position, query_sum, [], group, pieces, held_second, layouts[0], aligned
            )
        ]
        held_second, layouts = last_second, layouts[1]
    else:
        held_second, layouts = held_second + last_second, layouts[0] + layouts[1]
    landed = [lax.ppermute(sent, "expert", flip(group, d * CORES)) for d in others]
    partial = score_call(
        position,
        query_sum,
        [small_mask, membership, chosen, *landed, *before],
        group,
        pieces,
        held_second,
        layouts,
        aligned,
    )
    scores = partial[0]
    for d in range(1, group):
        scores = scores + lax.ppermute(partial[d], "expert", flip(group, d))
    return scores


def solution(mesh):
    return jax.shard_map(
        per_device,
        mesh=mesh,
        in_specs=(
            P(("dp", "expert"), None),
            P(("dp", "expert"), None, None),
            P(("dp", "expert"), None),
            P(("dp", "expert"), None),
            P("expert", None, "dp"),
            P("expert", None, "dp"),
            P("expert", "dp", None),
            P("expert", "dp", None),
        ),
        out_specs=P(("dp", "expert"), None),
        check_vma=False,
    )
```

```python
import functools

import jax
import jax.numpy as jnp
import numpy as np
from jax import lax
from jax.experimental import pallas as pl
from jax.experimental.pallas import tpu as pltpu
from jax.sharding import PartitionSpec as P

RANK = 32
SEG_DEV = 4
CORES = 2
TOP_EXPONENT = 15.0
TAIL = 16


def bits_of(count):
    return (count - 1).bit_length()


def slot_order(order):
    width = len(order)
    return [
        sum(((slot >> (width - 1 - i)) & 1) << bit for i, bit in enumerate(order))
        for slot in range(1 << width)
    ]


def column_exponent(query):
    peak = jnp.max(jnp.abs(query).astype(jnp.float32), axis=0, keepdims=True)
    bound = jnp.maximum(peak * (0.25 * query.shape[0]), 1e-28)
    return jnp.floor(jnp.log2(bound)) + 1.0


def fold_kernel(width, steps, scaled, *refs):
    basis_refs, refs = refs[1 : 1 + 2 * width], refs[1 + 2 * width :]
    query_refs, out_refs, sum_refs, done = refs[:2], refs[2:4], refs[4:6], refs[6]
    step = pl.program_id(0)
    for chunk in range(2):
        query_ref, out_ref, sum_ref = query_refs[chunk], out_refs[chunk], sum_refs[chunk]
        chunk_refs = basis_refs[chunk * width : (chunk + 1) * width]
        rows = chunk_refs[0].shape[0]

        def piece(index):
            here = pl.ds(index * (width * rows), width * rows)
            return pltpu.make_async_copy(
                sum_ref.at[here, :], out_ref.at[here, :], done.at[chunk, index]
            )

        here = pl.ds(steps * width * rows, TAIL)
        tail = pltpu.make_async_copy(
            sum_ref.at[here, :], out_ref.at[here, :], done.at[chunk, steps]
        )
        for index in range(steps):

            @pl.when(step == chunk * steps + index)
            def _():
                exponent = column_exponent(query_ref[...])
                for part, basis_ref in enumerate(chunk_refs):
                    terms = jnp.dot(
                        basis_ref[...], query_ref[...], preferred_element_type=jnp.float32
                    )
                    if scaled:
                        terms = terms * jnp.exp2(TOP_EXPONENT - exponent)
                    sum_ref[pl.ds((index * width + part) * rows, rows), :] = terms
                piece(index).start()
                if index == 0:
                    sum_ref[here, :] = jnp.broadcast_to(exponent, (TAIL, sum_ref.shape[1]))
                    tail.start()

        @pl.when(step == 2 * steps - 1)
        def _():
            for index in range(steps):
                piece(index).wait()
            tail.wait()


def fold_parts(bases, queries, position, orders, halves, upper):
    columns = queries[0].shape[1]
    blocks = 1 << len(orders[0])
    count = blocks * halves
    width = min(4, count // 2)
    steps = count // 2 // width

    def block(chunk, part):
        order, basis = orders[chunk], bases[chunk]

        def index(i, position_ref):
            i = jnp.clip(i - chunk * steps, 0, steps - 1)
            slot = (i * width + part) // halves + (blocks // 2 if upper else 0)
            relative = sum(
                ((slot >> (len(order) - 1 - n)) & 1) << bit for n, bit in enumerate(order)
            )
            here = (i * width + part) % halves ^ position_ref[1]
            return here * blocks + (relative ^ position_ref[0]), 0

        return pl.BlockSpec((basis.shape[0] // count, basis.shape[1]), index)

    out_shape = [
        jax.ShapeDtypeStruct((basis.shape[0] // 2 + TAIL, columns), jnp.float32)
        for basis in bases
    ]
    return pl.pallas_call(
        functools.partial(fold_kernel, width, steps, upper),
        grid_spec=pltpu.PrefetchScalarGridSpec(
            num_scalar_prefetch=1,
            grid=(2 * steps,),
            in_specs=[block(chunk, part) for chunk in range(2) for part in range(width)]
            + [pl.BlockSpec(query.shape, lambda i, p: (0, 0)) for query in queries],
            out_specs=[pl.BlockSpec(memory_space=pl.ANY)] * 2,
            scratch_shapes=[pltpu.VMEM(out.shape, out.dtype) for out in out_shape]
            + [pltpu.SemaphoreType.DMA((2, steps + 1))],
        ),
        out_shape=out_shape,
        compiler_params=pltpu.CompilerParams(vmem_limit_bytes=56 * 1024 * 1024),
        cost_estimate=pl.CostEstimate(flops=1, bytes_accessed=1, transcendentals=0),
    )(position, *([bases[0]] * width), *([bases[1]] * width), *queries)


def pack(keep, landed, there, exponent):
    half = (keep.shape[0] - TAIL) // 2
    values = landed[half:].astype(jnp.float32) * jnp.exp2(there - TOP_EXPONENT)
    scaled = (keep[half:] + values) * jnp.exp2(TOP_EXPONENT - exponent)
    row = lax.broadcasted_iota(jnp.int32, scaled.shape, 0)
    return jnp.where(row < half, scaled, exponent).astype(jnp.float16)


def flip(size, mask):
    return [(i, i ^ mask) for i in range(size)]


def tie(*values):
    return lax.optimization_barrier(values)


def column_kernel(halves, position_ref, source_ref, extra_ref, *out_refs):
    width = source_ref.shape[1]
    for d in range(halves):

        @pl.when(pl.program_id(0) == d)
        def _():
            out_refs[d][:, pl.ds(0, width)] = source_ref[...]
            out_refs[d][:, pl.ds(width, extra_ref.shape[1])] = extra_ref[...]


def column_parts(source, extra, position, halves):
    rows, width = source.shape[0], source.shape[1] // halves
    out_shape = (rows, width + extra.shape[1])
    return pl.pallas_call(
        functools.partial(column_kernel, halves),
        grid_spec=pltpu.PrefetchScalarGridSpec(
            num_scalar_prefetch=1,
            grid=(halves,),
            in_specs=[
                pl.BlockSpec((rows, width), lambda j, p: (0, p[1] ^ j)),
                pl.BlockSpec(extra.shape, lambda j, p: (0, 0)),
            ],
            out_specs=[pl.BlockSpec(out_shape, lambda j, p: (0, 0))] * halves,
        ),
        out_shape=[jax.ShapeDtypeStruct(out_shape, source.dtype)] * halves,
        compiler_params=pltpu.CompilerParams(vmem_limit_bytes=56 * 1024 * 1024),
        cost_estimate=pl.CostEstimate(flops=1, bytes_accessed=1, transcendentals=0),
    )(position, source, extra)


def flatten_kernel(position_ref, source_ref, *out_refs):
    rows, width = out_refs[0].shape
    for d, out_ref in enumerate(out_refs):
        start = pl.multiple_of((position_ref[1] ^ d) * width, width)
        out_ref[...] = source_ref[:, :, pl.ds(start, width)].reshape(rows, width)


def flattened_parts(source, position, halves):
    tokens, top, width = source.shape
    block = 32
    out = (tokens * top, width // halves)
    own, *away = pl.pallas_call(
        flatten_kernel,
        grid_spec=pltpu.PrefetchScalarGridSpec(
            num_scalar_prefetch=1,
            grid=(tokens // block,),
            in_specs=[pl.BlockSpec((block, top, width), lambda i, p: (i, 0, 0))],
            out_specs=[pl.BlockSpec((block * top, out[1]), lambda i, p: (i, 0))] * halves,
        ),
        out_shape=[jax.ShapeDtypeStruct(out, source.dtype)] * halves,
        compiler_params=pltpu.CompilerParams(vmem_limit_bytes=56 * 1024 * 1024),
        cost_estimate=pl.CostEstimate(
            flops=1, bytes_accessed=4 * source.size, transcendentals=0
        ),
    )(position, source)
    return own, away


def start_all(copies, done):
    started = []
    for i, (source, target) in enumerate(copies):
        started.append(pltpu.make_async_copy(source, target, done.at[i]))
        started[i].start()
    return started


def mask_kernel(top, position_ref, *refs):
    *extra_refs, mask_ref, small_mask_ref, member_ref, rows_ref = refs
    tokens, lanes = extra_refs[0].shape
    lane = lax.broadcasted_iota(jnp.int32, (tokens, lanes), 1).astype(jnp.float32)
    for i, extra_ref in enumerate(extra_refs):
        extra = extra_ref[...].astype(jnp.float32)

        def column(k):
            return jnp.broadcast_to(extra[:, k : k + 1], (tokens, lanes))

        member = jnp.where(column(top) + float(i * SEG_DEV) == lane, 1.0, 0.0)
        for k in range(top):
            rows = pl.ds(i * tokens * top + k, tokens, stride=top)
            rows_ref[rows, :] = member
            for d in range(mask_ref.shape[0]):
                expert = ((position_ref[1] ^ d) * CORES + position_ref[2]).astype(jnp.float32)
                mask_ref[d, rows, :] = jnp.where(column(k) == expert, 1.0, 0.0)
    member_ref[...] = rows_ref[...].astype(member_ref.dtype)
    small_mask_ref[...] = mask_ref[...].astype(small_mask_ref.dtype)


def masks(position, pieces, top, halves, lanes):
    tokens = pieces[0].shape[0]
    rows = len(pieces) * tokens * top
    last = pieces[0].shape[1] // lanes - 1
    return pl.pallas_call(
        functools.partial(mask_kernel, top),
        grid=(1,),
        in_specs=[pl.BlockSpec(memory_space=pltpu.SMEM)]
        + [pl.BlockSpec((tokens, lanes), lambda i: (0, last))] * len(pieces),
        out_specs=[
            pl.BlockSpec((halves, rows, lanes), lambda i: (0, 0, 0)),
            pl.BlockSpec((halves, rows, lanes), lambda i: (0, 0, 0)),
            pl.BlockSpec((rows, lanes), lambda i: (0, 0)),
        ],
        out_shape=[
            jax.ShapeDtypeStruct((halves, rows, lanes), jnp.float32),
            jax.ShapeDtypeStruct((halves, rows, lanes), jnp.bfloat16),
            jax.ShapeDtypeStruct((rows, lanes), jnp.bfloat16),
        ],
        scratch_shapes=[pltpu.VMEM((rows, lanes), jnp.float32)],
        cost_estimate=pl.CostEstimate(flops=1, bytes_accessed=1, transcendentals=0),
    )(position, *pieces)


def input_kernel(top, layouts, count, position_ref, mask_in_ref, *refs):
    *refs, out_ref, sent_ref, tokens_ref, held_ref, mask_ref, done = refs
    token_refs, fold_refs = refs[:count], refs[count:]
    rows = token_refs[0].shape[0]
    copies = [
        (token_ref.at[:, pl.ds(0, tokens_ref.shape[1])], tokens_ref.at[pl.ds(i * rows, rows), :])
        for i, token_ref in enumerate(token_refs)
    ]
    for fold_ref, (relatives, offset, block) in zip(fold_refs, layouts):
        rows = fold_ref.shape[1]
        for slot, relative in enumerate(relatives):
            start = pl.multiple_of((relative ^ position_ref[0]) * block + offset, 16)
            copies.append((fold_ref.at[slot], held_ref.at[pl.ds(start, rows), :]))
    *copies, mask_copy = start_all(copies + [(mask_in_ref, mask_ref)], done)
    for copy in copies:
        copy.wait()
    terms = jnp.dot(tokens_ref[...], held_ref[...], preferred_element_type=jnp.float32)
    mask_copy.wait()
    total = tokens_ref.shape[0]
    columns = out_ref.shape[1]
    for k in range(top):
        rows_of = pl.ds(k, total, stride=top)
        out_ref[rows_of, :] = sum(
            terms[:, d * columns : (d + 1) * columns] * mask_ref[d, rows_of, :]
            for d in range(mask_ref.shape[0])
        )
    sent_ref[...] = out_ref[...].astype(sent_ref.dtype)


def input_chosen(position, pieces, held, orders, mask, top):
    total = sum(piece.shape[0] for piece in pieces)
    columns = mask.shape[2]
    width, across = pieces[0].shape[1] - columns, held[0].shape[2]
    block = sum(part.shape[1] for part in held[0::2])
    layouts, offset = [], 0
    for first, last, order in zip(held[0::2], held[1::2], orders):
        relatives = slot_order(order)
        middle = first.shape[0]
        layouts += [(relatives[:middle], offset, block), (relatives[middle:], offset, block)]
        offset += first.shape[1]
    slots = sum(part.shape[0] for part in held)
    return pl.pallas_call(
        functools.partial(input_kernel, top, layouts, len(pieces)),
        in_specs=[pl.BlockSpec(memory_space=pltpu.SMEM)]
        + [pl.BlockSpec(memory_space=pl.ANY)] * (1 + len(pieces) + len(held)),
        out_specs=[pl.BlockSpec(memory_space=pltpu.VMEM)] * 2,
        out_shape=[
            jax.ShapeDtypeStruct((total * top, columns), jnp.float32),
            jax.ShapeDtypeStruct((total * top, columns), jnp.bfloat16),
        ],
        scratch_shapes=[
            pltpu.VMEM((total, width), pieces[0].dtype),
            pltpu.VMEM((width, across), held[0].dtype),
            pltpu.VMEM(mask.shape, mask.dtype),
            pltpu.SemaphoreType.DMA((len(pieces) + slots + 1,)),
        ],
        compiler_params=pltpu.CompilerParams(vmem_limit_bytes=58 * 1024 * 1024),
        cost_estimate=pl.CostEstimate(flops=1, bytes_accessed=1, transcendentals=0),
    )(position, mask, *pieces, *held)


def spans(counts):
    starts = [sum(counts[:i]) for i in range(len(counts))]
    return list(zip(starts, counts))


def output_terms(position_ref, layouts, aligned, token_refs, fold_refs, buffers):
    tokens_ref, fold_ref, total_ref, folded, done = buffers
    counts = [token_ref.shape[0] for token_ref in token_refs]
    fold_copies, token_copies, row = [], [], 0
    for held_ref, (relatives, part, size) in zip(fold_refs, layouts):
        rows = held_ref.shape[1]
        for slot, relative in enumerate(relatives):
            block = (relative ^ position_ref[0]) * size + part
            target = row if aligned else pl.multiple_of(block * rows, rows)
            fold_copies.append((held_ref.at[slot], fold_ref.at[pl.ds(target, rows), :]))
            if aligned:
                across = pl.ds(row, rows)
                token_copies.append(
                    [
                        (
                            token_ref.at[:, pl.ds(pl.multiple_of(block * rows, rows), rows)],
                            tokens_ref.at[pl.ds(first, count), across],
                        )
                        for token_ref, (first, count) in zip(token_refs, spans(counts))
                    ]
                )
            row += rows
    if not aligned:
        token_copies = [
            [
                (token_ref, tokens_ref.at[pl.ds(first, count), :])
                for token_ref, (first, count) in zip(token_refs, spans(counts))
            ]
        ]
    fold_copies = start_all(fold_copies, folded)
    token_copies = [start_all(copies, done.at[i]) for i, copies in enumerate(token_copies)]
    for copy in fold_copies:
        copy.wait()
    for copies in token_copies:
        for copy in copies:
            copy.wait()
    total_ref[...] = jnp.dot(
        tokens_ref[...], fold_ref[...], preferred_element_type=jnp.float32
    )


def first_kernel(layouts, count, position_ref, *refs):
    token_refs, refs = refs[:count], refs[count:]
    *fold_refs, total_ref, tokens_ref, fold_ref, folded, done = refs
    buffers = tokens_ref, fold_ref, total_ref, folded, done
    output_terms(position_ref, layouts, True, token_refs, fold_refs, buffers)


def last_kernel(layouts, aligned, count, extra_count, group, position_ref, *refs):
    query_ref, *refs = refs
    extra_refs, refs = refs[:extra_count], refs[extra_count:]
    token_refs, refs = refs[:count], refs[count:]
    held_refs, refs = refs[-extra_count:], refs[:-extra_count]
    fold_refs, refs = refs[: len(layouts)], refs[len(layouts) :]
    out_refs, (tokens_ref, fold_ref, total_ref, folded, done, extra_done) = refs[:group], refs[group:]
    extra_copies = start_all(list(zip(extra_refs, held_refs)), extra_done)
    buffers = tokens_ref, fold_ref, total_ref, folded, done
    output_terms(position_ref, layouts, aligned, token_refs, fold_refs, buffers)
    for copy in extra_copies:
        copy.wait()
    mask_ref, member_ref, chosen_ref, *refs = held_refs
    halves = mask_ref.shape[0]
    landed_refs, before_refs = refs[: halves - 1], refs[halves - 1 :]
    columns = chosen_ref.shape[1]
    rows = chosen_ref.shape[0] // halves
    summed = 0.0
    for h in range(halves):
        here = pl.ds(h * rows, rows)
        inputs = chosen_ref[here, :]
        for d, landed_ref in enumerate(landed_refs):
            landed = landed_ref[pl.ds((h ^ (d + 1)) * rows, rows), :]
            inputs = inputs + landed.astype(jnp.float32)
        total = total_ref[here, :]
        for before_ref in before_refs:
            total = total + before_ref[here, :]
        products = inputs * sum(
            total[:, d * columns : (d + 1) * columns] * mask_ref[d, here, :].astype(jnp.float32)
            for d in range(halves)
        )
        high = products.astype(jnp.bfloat16)
        low = (products - high.astype(jnp.float32)).astype(jnp.bfloat16)
        for part in (high, low):
            summed = summed + lax.dot_general(
                member_ref[here, :],
                part,
                (((0,), (0,)), ((), ())),
                preferred_element_type=jnp.float32,
            )
    scores = jnp.dot(
        summed,
        query_ref[...],
        precision=lax.Precision.HIGHEST,
        preferred_element_type=jnp.float32,
    )
    for i, out_ref in enumerate(out_refs):
        out_ref[...] = scores[i * SEG_DEV : (i + 1) * SEG_DEV]


def score_call(position, query_sum, extras, group, pieces, folds, layouts, aligned):
    total = sum(piece.shape[0] for piece in pieces)
    across = folds[0].shape[2]
    width = sum(fold.shape[0] * fold.shape[1] for fold in folds)
    slots = sum(fold.shape[0] for fold in folds)
    vmem, anywhere = pl.BlockSpec(memory_space=pltpu.VMEM), pl.BlockSpec(memory_space=pl.ANY)
    smem = pl.BlockSpec(memory_space=pltpu.SMEM)
    totals = jax.ShapeDtypeStruct((total, across), jnp.float32)
    semaphores = [
        pltpu.SemaphoreType.DMA((slots,)),
        pltpu.SemaphoreType.DMA((slots if aligned else 1, len(pieces))),
    ]
    buffers = [
        pltpu.VMEM((total, width), pieces[0].dtype),
        pltpu.VMEM((width, across), folds[0].dtype),
    ]
    options = dict(
        compiler_params=pltpu.CompilerParams(vmem_limit_bytes=58 * 1024 * 1024),
        cost_estimate=pl.CostEstimate(
            flops=1,
            bytes_accessed=1 if extras else 2 * (total + across) * width,
            transcendentals=0,
        ),
    )
    if not extras:
        return pl.pallas_call(
            functools.partial(first_kernel, layouts, len(pieces)),
            in_specs=[smem] + [anywhere] * (len(pieces) + len(folds)),
            out_specs=vmem,
            out_shape=totals,
            scratch_shapes=buffers + semaphores,
            **options,
        )(position, *pieces, *folds)
    scores = jax.ShapeDtypeStruct((SEG_DEV, query_sum.shape[1]), jnp.float32)
    return pl.pallas_call(
        functools.partial(last_kernel, layouts, aligned, len(pieces), len(extras), group),
        in_specs=[smem, vmem] + [anywhere] * (len(extras) + len(pieces) + len(folds)),
        out_specs=[vmem] * group,
        out_shape=[scores] * group,
        scratch_shapes=buffers
        + [pltpu.VMEM(totals.shape, jnp.float32)]
        + semaphores
        + [pltpu.SemaphoreType.DMA((len(extras),))]
        + [pltpu.VMEM(extra.shape, extra.dtype) for extra in extras],
        **options,
    )(position, query_sum, *extras, *pieces, *folds)


def output_layouts(orders):
    sides = [[], []]
    for n, order in enumerate(orders):
        relatives = slot_order(order)
        middle = len(relatives) // 2
        sides[0].append((relatives[:middle], n, len(orders)))
        sides[1].append((relatives[middle:], n, len(orders)))
    return sides


def per_device(
    activations,
    gate_gradient,
    routes,
    sequence_ids,
    input_basis,
    output_basis,
    input_query,
    output_query,
):
    blocks = lax.axis_size("dp")
    group = lax.axis_size("expert")
    halves = group // CORES
    place = lax.axis_index("dp")
    member = lax.axis_index("expert")
    half = member // CORES
    core = member % CORES
    tokens, top = routes.shape
    columns = input_query.shape[2]
    queries = columns // RANK
    count = bits_of(blocks)

    def send(packed, bit):
        return lax.ppermute(packed, "dp", flip(blocks, 1 << bit))

    def joined(keep, landed, exponent):
        half = (keep.shape[0] - TAIL) // 2
        there = landed[2 * half : 2 * half + 1].astype(jnp.float32)
        exponent = jnp.maximum(exponent, there) + 1
        packed = pack(keep, landed, there, exponent)
        here = slice(0, half + TAIL)
        values = landed[here].astype(jnp.float32) * jnp.exp2(there - TOP_EXPONENT)
        return packed, exponent, keep[here] + values

    def own_shard(keep, landed):
        rows = keep.shape[0] - TAIL
        there = landed[rows : rows + 1].astype(jnp.float32)
        values = landed[:rows].astype(jnp.float32) * jnp.exp2(there - TOP_EXPONENT)
        return (keep[:rows] + values).astype(jnp.bfloat16).reshape(halves, -1, columns)

    def exchange(shard):
        pieces = [shard[0]] + [
            lax.ppermute(shard[d], "expert", flip(group, d * CORES)) for d in range(1, halves)
        ]
        return jnp.concatenate(pieces, axis=1)

    def from_half(part, d):
        return part if d == 0 else lax.ppermute(part, "expert", flip(group, d * CORES))

    def from_core(part):
        return lax.ppermute(part, "expert", flip(group, 1))

    order_second = list(range(count))
    order_first = order_second[1::-1] + order_second[2:]
    position = jnp.stack([place, half, core]).astype(jnp.int32)

    def parts(bases, upper):
        queries = (input_query[0], output_query[0])
        return fold_parts(bases, queries, position, (order_first, order_second), halves, upper)

    bases = input_basis[0], output_basis[0]
    packed_first, packed_second = [part.astype(jnp.float16) for part in parts(bases, True)]
    *bases, packed_first, packed_second = tie(*bases, packed_first, packed_second)
    landed_first = send(packed_first, order_first[0])
    landed_second = send(packed_second, order_second[0])
    exponent_first = column_exponent(input_query[0])
    exponent_second = column_exponent(output_query[0])

    others = range(1, halves)
    gather_orders = [order_second, order_second[1:] + order_second[:1]]
    keep_first, keep_second = parts(bases, False)
    activations, keep_first = tie(activations, keep_first)
    extra = jnp.concatenate([routes, sequence_ids.T], axis=1).astype(jnp.bfloat16)
    extra = jnp.pad(extra, ((0, 0), (0, columns - extra.shape[1])))
    input_parts = list(column_parts(activations, extra, position, halves))
    landed_first, *input_parts = tie(landed_first, *input_parts)
    input_parts = [from_half(part, d) for d, part in enumerate(input_parts)]

    packed_first, exponent_first, keep_first = joined(keep_first, landed_first, exponent_first)
    landed_first = send(packed_first, order_first[1])
    packed_second, exponent_second, keep_second = joined(
        keep_second, landed_second, exponent_second
    )
    gate_gradient, packed_second = tie(gate_gradient, packed_second)
    landed_second = send(packed_second, order_second[1])
    own_gradient, away = flattened_parts(gate_gradient, position, halves)
    landed_first, own_gradient = tie(landed_first, own_gradient)

    for bit in order_first[2:]:
        packed_first, exponent_first, keep_first = joined(
            keep_first, landed_first, exponent_first
        )
        landed_first = send(packed_first, bit)
    for bit in order_second[2:]:
        packed_second, exponent_second, keep_second = joined(
            keep_second, landed_second, exponent_second
        )
        keep_second, landed_first = tie(keep_second, landed_first)
        landed_second = send(packed_second, bit)
    own_half, *input_parts = input_parts
    shard_first, *input_parts = tie(own_shard(keep_first, landed_first), *input_parts)
    input_pieces = [own_half, from_core(own_half)]
    for part in input_parts:
        input_pieces += [part, from_core(part)]
    swapped_gradient = from_core(own_gradient)
    mask, small_mask, membership = masks(position, input_pieces, top, halves, columns)
    query_sum = jnp.asarray(
        np.arange(columns)[:, None] // RANK == np.arange(queries)[None, :], jnp.float32
    )

    def split(shard):
        cut = (shard.shape[0] // len(gather_orders) + 15) // 16 * 16
        return [shard[:cut][None], shard[cut:][None]]

    def stage_of(held, stage):
        return [send(part, bits[stage]) for part, bits in zip(held, gather_orders)]

    def both(held, landed):
        return [jnp.concatenate(pair) for pair in zip(held, landed)]

    shard_first = exchange(shard_first)
    shard_first, landed_second = tie(shard_first, landed_second)
    held_first = shard_first[None]
    landed_first = send(held_first, order_second[-1])
    shard_second = exchange(own_shard(keep_second, landed_second))
    shard_second, *away = tie(shard_second, *away)
    landed_first, mask, small_mask, membership, swapped_gradient = tie(
        landed_first, mask, small_mask, membership, swapped_gradient
    )
    held_first = jnp.concatenate([held_first, landed_first])
    away = [from_half(part, d) for d, part in zip(others, away)]
    held_second = split(shard_second)
    for stage in range(2, count):
        landed_first = send(held_first, order_second[-stage])
        landed = stage_of(held_second, 1 - stage)
        held_second = both(held_second, landed)
        landed_first, *held_second = tie(landed_first, *held_second)
        held_first = jnp.concatenate([held_first, landed_first])
    last_first = send(held_first, order_second[0])
    held_second = both(held_second, stage_of(held_second, 1 - count))
    last_second = stage_of(held_second, 0)
    last_first, *held_second = tie(last_first, *held_second)

    chosen, sent = input_chosen(
        position, input_pieces, [held_first, last_first], [order_second], mask, top
    )
    sent, *away = tie(sent, *away)
    pieces = [own_gradient, swapped_gradient]
    for part in away:
        pieces += [part, from_core(part)]
    layouts = output_layouts(gather_orders)
    aligned = held_second[0].shape[1] % 128 == 0
    before = []
    if aligned:
        sent, *held_second = tie(sent, *held_second)
        before = [
            score_call(
                position, query_sum, [], group, pieces, held_second, layouts[0], aligned
            )
        ]
        held_second, layouts = last_second, layouts[1]
    else:
        held_second, layouts = held_second + last_second, layouts[0] + layouts[1]
    landed = [lax.ppermute(sent, "expert", flip(group, d * CORES)) for d in others]
    partial = score_call(
        position,
        query_sum,
        [small_mask, membership, chosen, *landed, *before],
        group,
        pieces,
        held_second,
        layouts,
        aligned,
    )
    scores = partial[0]
    for d in range(1, group):
        scores = scores + lax.ppermute(partial[d], "expert", flip(group, d))
    return scores


def solution(mesh):
    return jax.shard_map(
        per_device,
        mesh=mesh,
        in_specs=(
            P(("dp", "expert"), None),
            P(("dp", "expert"), None, None),
            P(("dp", "expert"), None),
            P(("dp", "expert"), None),
            P("expert", None, "dp"),
            P("expert", None, "dp"),
            P("expert", "dp", None),
            P("expert", "dp", None),
        ),
        out_specs=P(("dp", "expert"), None),
        check_vma=False,
    )
```

```python
import functools

import jax
import jax.numpy as jnp
import numpy as np
from jax import lax
from jax.experimental import pallas as pl
from jax.experimental.pallas import tpu as pltpu
from jax.sharding import PartitionSpec as P

RANK = 32
SEG_DEV = 4
CORES = 2
TOP_EXPONENT = 15.0
TAIL = 16


def bits_of(count):
    return (count - 1).bit_length()


def slot_order(order):
    width = len(order)
    return [
        sum(((slot >> (width - 1 - i)) & 1) << bit for i, bit in enumerate(order))
        for slot in range(1 << width)
    ]


def column_exponent(query):
    peak = jnp.max(jnp.abs(query).astype(jnp.float32), axis=0, keepdims=True)
    bound = jnp.maximum(peak * (0.25 * query.shape[0]), 1e-28)
    return jnp.floor(jnp.log2(bound)) + 1.0


def fold_kernel(width, steps, scaled, *refs):
    basis_refs, refs = refs[1 : 1 + 2 * width], refs[1 + 2 * width :]
    query_refs, out_refs, sum_refs, done = refs[:2], refs[2:4], refs[4:6], refs[6]
    step = pl.program_id(0)
    for chunk in range(2):
        query_ref, out_ref, sum_ref = query_refs[chunk], out_refs[chunk], sum_refs[chunk]
        chunk_refs = basis_refs[chunk * width : (chunk + 1) * width]
        rows = chunk_refs[0].shape[0]

        def piece(index):
            here = pl.ds(index * (width * rows), width * rows)
            return pltpu.make_async_copy(
                sum_ref.at[here, :], out_ref.at[here, :], done.at[chunk, index]
            )

        here = pl.ds(steps * width * rows, TAIL)
        tail = pltpu.make_async_copy(
            sum_ref.at[here, :], out_ref.at[here, :], done.at[chunk, steps]
        )
        for index in range(steps):

            @pl.when(step == chunk * steps + index)
            def _():
                exponent = column_exponent(query_ref[...])
                for part, basis_ref in enumerate(chunk_refs):
                    terms = jnp.dot(
                        basis_ref[...], query_ref[...], preferred_element_type=jnp.float32
                    )
                    if scaled:
                        terms = terms * jnp.exp2(TOP_EXPONENT - exponent)
                    sum_ref[pl.ds((index * width + part) * rows, rows), :] = terms
                piece(index).start()
                if index == 0:
                    sum_ref[here, :] = jnp.broadcast_to(exponent, (TAIL, sum_ref.shape[1]))
                    tail.start()

        @pl.when(step == 2 * steps - 1)
        def _():
            for index in range(steps):
                piece(index).wait()
            tail.wait()


def fold_parts(bases, queries, position, orders, halves, upper):
    columns = queries[0].shape[1]
    blocks = 1 << len(orders[0])
    count = blocks * halves
    width = min(4, count // 2)
    steps = count // 2 // width

    def block(chunk, part):
        order, basis = orders[chunk], bases[chunk]

        def index(i, position_ref):
            i = jnp.clip(i - chunk * steps, 0, steps - 1)
            slot = (i * width + part) // halves + (blocks // 2 if upper else 0)
            relative = sum(
                ((slot >> (len(order) - 1 - n)) & 1) << bit for n, bit in enumerate(order)
            )
            here = (i * width + part) % halves ^ position_ref[1]
            return here * blocks + (relative ^ position_ref[0]), 0

        return pl.BlockSpec((basis.shape[0] // count, basis.shape[1]), index)

    out_shape = [
        jax.ShapeDtypeStruct((basis.shape[0] // 2 + TAIL, columns), jnp.float32)
        for basis in bases
    ]
    return pl.pallas_call(
        functools.partial(fold_kernel, width, steps, upper),
        grid_spec=pltpu.PrefetchScalarGridSpec(
            num_scalar_prefetch=1,
            grid=(2 * steps,),
            in_specs=[block(chunk, part) for chunk in range(2) for part in range(width)]
            + [pl.BlockSpec(query.shape, lambda i, p: (0, 0)) for query in queries],
            out_specs=[pl.BlockSpec(memory_space=pl.ANY)] * 2,
            scratch_shapes=[pltpu.VMEM(out.shape, out.dtype) for out in out_shape]
            + [pltpu.SemaphoreType.DMA((2, steps + 1))],
        ),
        out_shape=out_shape,
        compiler_params=pltpu.CompilerParams(vmem_limit_bytes=56 * 1024 * 1024),
        cost_estimate=pl.CostEstimate(flops=1, bytes_accessed=1, transcendentals=0),
    )(position, *([bases[0]] * width), *([bases[1]] * width), *queries)


def pack(keep, landed, there, exponent):
    half = (keep.shape[0] - TAIL) // 2
    values = landed[half:].astype(jnp.float32) * jnp.exp2(there - TOP_EXPONENT)
    scaled = (keep[half:] + values) * jnp.exp2(TOP_EXPONENT - exponent)
    row = lax.broadcasted_iota(jnp.int32, scaled.shape, 0)
    return jnp.where(row < half, scaled, exponent).astype(jnp.float16)


def flip(size, mask):
    return [(i, i ^ mask) for i in range(size)]


def tie(*values):
    return lax.optimization_barrier(values)


def column_kernel(halves, position_ref, source_ref, extra_ref, *out_refs):
    width = source_ref.shape[1]
    for d in range(halves):

        @pl.when(pl.program_id(0) == d)
        def _():
            out_refs[d][:, pl.ds(0, width)] = source_ref[...]
            out_refs[d][:, pl.ds(width, extra_ref.shape[1])] = extra_ref[...]


def column_parts(source, extra, position, halves):
    rows, width = source.shape[0], source.shape[1] // halves
    out_shape = (rows, width + extra.shape[1])
    return pl.pallas_call(
        functools.partial(column_kernel, halves),
        grid_spec=pltpu.PrefetchScalarGridSpec(
            num_scalar_prefetch=1,
            grid=(halves,),
            in_specs=[
                pl.BlockSpec((rows, width), lambda j, p: (0, p[1] ^ j)),
                pl.BlockSpec(extra.shape, lambda j, p: (0, 0)),
            ],
            out_specs=[pl.BlockSpec(out_shape, lambda j, p: (0, 0))] * halves,
        ),
        out_shape=[jax.ShapeDtypeStruct(out_shape, source.dtype)] * halves,
        compiler_params=pltpu.CompilerParams(vmem_limit_bytes=56 * 1024 * 1024),
        cost_estimate=pl.CostEstimate(flops=1, bytes_accessed=1, transcendentals=0),
    )(position, source, extra)


def flatten_kernel(halves, position_ref, source_ref, *out_refs):
    step = pl.program_id(0)
    rows, width = out_refs[0].shape
    for d in range(halves):
        start = pl.multiple_of((position_ref[1] ^ d) * width, width)
        part = source_ref[:, :, pl.ds(start, width)].reshape(rows, width)
        if d == 0:
            out_refs[0][...] = part
            continue

        @pl.when(step == 0)
        def _():
            out_refs[2 * d - 1][...] = part

        @pl.when(step > 0)
        def _():
            out_refs[2 * d][...] = part


def flattened_parts(source, position, halves):
    tokens, top, width = source.shape
    block = 32
    rows, width = block * top, width // halves
    shapes = [tokens * top] + [rows, tokens * top - rows] * (halves - 1)
    specs = [
        pl.BlockSpec((rows, width), lambda i, p: (i, 0)),
        pl.BlockSpec((rows, width), lambda i, p: (0, 0)),
        pl.BlockSpec((rows, width), lambda i, p: (jnp.maximum(i - 1, 0), 0)),
    ]
    own, *away = pl.pallas_call(
        functools.partial(flatten_kernel, halves),
        grid_spec=pltpu.PrefetchScalarGridSpec(
            num_scalar_prefetch=1,
            grid=(tokens // block,),
            in_specs=[pl.BlockSpec((block,) + source.shape[1:], lambda i, p: (i, 0, 0))],
            out_specs=specs[:1] + specs[1:] * (halves - 1),
        ),
        out_shape=[jax.ShapeDtypeStruct((count, width), source.dtype) for count in shapes],
        compiler_params=pltpu.CompilerParams(vmem_limit_bytes=56 * 1024 * 1024),
        cost_estimate=pl.CostEstimate(
            flops=1, bytes_accessed=4 * source.size, transcendentals=0
        ),
    )(position, source)
    return own, away[0::2], away[1::2]


def start_all(copies, done):
    started = []
    for i, (source, target) in enumerate(copies):
        started.append(pltpu.make_async_copy(source, target, done.at[i]))
        started[i].start()
    return started


def mask_kernel(top, position_ref, *refs):
    *extra_refs, mask_ref, small_mask_ref, member_ref, rows_ref = refs
    tokens, lanes = extra_refs[0].shape
    lane = lax.broadcasted_iota(jnp.int32, (tokens, lanes), 1).astype(jnp.float32)
    for i, extra_ref in enumerate(extra_refs):
        extra = extra_ref[...].astype(jnp.float32)

        def column(k):
            return jnp.broadcast_to(extra[:, k : k + 1], (tokens, lanes))

        member = jnp.where(column(top) + float(i * SEG_DEV) == lane, 1.0, 0.0)
        for k in range(top):
            rows = pl.ds(i * tokens * top + k, tokens, stride=top)
            rows_ref[rows, :] = member
            for d in range(mask_ref.shape[0]):
                expert = ((position_ref[1] ^ d) * CORES + position_ref[2]).astype(jnp.float32)
                mask_ref[d, rows, :] = jnp.where(column(k) == expert, 1.0, 0.0)
    member_ref[...] = rows_ref[...].astype(member_ref.dtype)
    small_mask_ref[...] = mask_ref[...].astype(small_mask_ref.dtype)


def masks(position, pieces, top, halves, lanes):
    tokens = pieces[0].shape[0]
    rows = len(pieces) * tokens * top
    last = pieces[0].shape[1] // lanes - 1
    return pl.pallas_call(
        functools.partial(mask_kernel, top),
        grid=(1,),
        in_specs=[pl.BlockSpec(memory_space=pltpu.SMEM)]
        + [pl.BlockSpec((tokens, lanes), lambda i: (0, last))] * len(pieces),
        out_specs=[
            pl.BlockSpec((halves, rows, lanes), lambda i: (0, 0, 0)),
            pl.BlockSpec((halves, rows, lanes), lambda i: (0, 0, 0)),
            pl.BlockSpec((rows, lanes), lambda i: (0, 0)),
        ],
        out_shape=[
            jax.ShapeDtypeStruct((halves, rows, lanes), jnp.float32),
            jax.ShapeDtypeStruct((halves, rows, lanes), jnp.bfloat16),
            jax.ShapeDtypeStruct((rows, lanes), jnp.bfloat16),
        ],
        scratch_shapes=[pltpu.VMEM((rows, lanes), jnp.float32)],
        cost_estimate=pl.CostEstimate(flops=1, bytes_accessed=1, transcendentals=0),
    )(position, *pieces)


def input_kernel(top, layouts, count, position_ref, mask_in_ref, *refs):
    *refs, out_ref, sent_ref, tokens_ref, held_ref, mask_ref, done = refs
    token_refs, fold_refs = refs[:count], refs[count:]
    rows = token_refs[0].shape[0]
    copies = [
        (token_ref.at[:, pl.ds(0, tokens_ref.shape[1])], tokens_ref.at[pl.ds(i * rows, rows), :])
        for i, token_ref in enumerate(token_refs)
    ]
    for fold_ref, (relatives, offset, block) in zip(fold_refs, layouts):
        rows = fold_ref.shape[1]
        for slot, relative in enumerate(relatives):
            start = pl.multiple_of((relative ^ position_ref[0]) * block + offset, 16)
            copies.append((fold_ref.at[slot], held_ref.at[pl.ds(start, rows), :]))
    *copies, mask_copy = start_all(copies + [(mask_in_ref, mask_ref)], done)
    for copy in copies:
        copy.wait()
    terms = jnp.dot(tokens_ref[...], held_ref[...], preferred_element_type=jnp.float32)
    mask_copy.wait()
    total = tokens_ref.shape[0]
    columns = out_ref.shape[1]
    for k in range(top):
        rows_of = pl.ds(k, total, stride=top)
        out_ref[rows_of, :] = sum(
            terms[:, d * columns : (d + 1) * columns] * mask_ref[d, rows_of, :]
            for d in range(mask_ref.shape[0])
        )
    sent_ref[...] = out_ref[...].astype(sent_ref.dtype)


def input_chosen(position, pieces, held, orders, mask, top):
    total = sum(piece.shape[0] for piece in pieces)
    columns = mask.shape[2]
    width, across = pieces[0].shape[1] - columns, held[0].shape[2]
    block = sum(part.shape[1] for part in held[0::2])
    layouts, offset = [], 0
    for first, last, order in zip(held[0::2], held[1::2], orders):
        relatives = slot_order(order)
        middle = first.shape[0]
        layouts += [(relatives[:middle], offset, block), (relatives[middle:], offset, block)]
        offset += first.shape[1]
    slots = sum(part.shape[0] for part in held)
    return pl.pallas_call(
        functools.partial(input_kernel, top, layouts, len(pieces)),
        in_specs=[pl.BlockSpec(memory_space=pltpu.SMEM)]
        + [pl.BlockSpec(memory_space=pl.ANY)] * (1 + len(pieces) + len(held)),
        out_specs=[pl.BlockSpec(memory_space=pltpu.VMEM)] * 2,
        out_shape=[
            jax.ShapeDtypeStruct((total * top, columns), jnp.float32),
            jax.ShapeDtypeStruct((total * top, columns), jnp.bfloat16),
        ],
        scratch_shapes=[
            pltpu.VMEM((total, width), pieces[0].dtype),
            pltpu.VMEM((width, across), held[0].dtype),
            pltpu.VMEM(mask.shape, mask.dtype),
            pltpu.SemaphoreType.DMA((len(pieces) + slots + 1,)),
        ],
        compiler_params=pltpu.CompilerParams(vmem_limit_bytes=58 * 1024 * 1024),
        cost_estimate=pl.CostEstimate(flops=1, bytes_accessed=1, transcendentals=0),
    )(position, mask, *pieces, *held)


def spans(counts):
    starts = [sum(counts[:i]) for i in range(len(counts))]
    return list(zip(starts, counts))


def output_terms(position_ref, layouts, aligned, token_refs, fold_refs, buffers):
    tokens_ref, fold_ref, total_ref, folded, done = buffers
    counts = [token_ref.shape[0] for token_ref in token_refs]
    fold_copies, token_copies, row = [], [], 0
    for held_ref, (relatives, part, size) in zip(fold_refs, layouts):
        rows = held_ref.shape[1]
        for slot, relative in enumerate(relatives):
            block = (relative ^ position_ref[0]) * size + part
            target = row if aligned else pl.multiple_of(block * rows, rows)
            fold_copies.append((held_ref.at[slot], fold_ref.at[pl.ds(target, rows), :]))
            if aligned:
                across = pl.ds(row, rows)
                token_copies.append(
                    [
                        (
                            token_ref.at[:, pl.ds(pl.multiple_of(block * rows, rows), rows)],
                            tokens_ref.at[pl.ds(first, count), across],
                        )
                        for token_ref, (first, count) in zip(token_refs, spans(counts))
                    ]
                )
            row += rows
    if not aligned:
        token_copies = [
            [
                (token_ref, tokens_ref.at[pl.ds(first, count), :])
                for token_ref, (first, count) in zip(token_refs, spans(counts))
            ]
        ]
    fold_copies = start_all(fold_copies, folded)
    token_copies = [start_all(copies, done.at[i]) for i, copies in enumerate(token_copies)]
    for copy in fold_copies:
        copy.wait()
    for copies in token_copies:
        for copy in copies:
            copy.wait()
    total_ref[...] = jnp.dot(
        tokens_ref[...], fold_ref[...], preferred_element_type=jnp.float32
    )


def first_kernel(layouts, count, position_ref, *refs):
    token_refs, refs = refs[:count], refs[count:]
    *fold_refs, total_ref, tokens_ref, fold_ref, folded, done = refs
    buffers = tokens_ref, fold_ref, total_ref, folded, done
    output_terms(position_ref, layouts, True, token_refs, fold_refs, buffers)


def last_kernel(layouts, aligned, count, extra_count, group, position_ref, *refs):
    query_ref, *refs = refs
    extra_refs, refs = refs[:extra_count], refs[extra_count:]
    token_refs, refs = refs[:count], refs[count:]
    held_refs, refs = refs[-extra_count:], refs[:-extra_count]
    fold_refs, refs = refs[: len(layouts)], refs[len(layouts) :]
    out_refs, (tokens_ref, fold_ref, total_ref, folded, done, extra_done) = refs[:group], refs[group:]
    extra_copies = start_all(list(zip(extra_refs, held_refs)), extra_done)
    buffers = tokens_ref, fold_ref, total_ref, folded, done
    output_terms(position_ref, layouts, aligned, token_refs, fold_refs, buffers)
    for copy in extra_copies:
        copy.wait()
    mask_ref, member_ref, chosen_ref, *refs = held_refs
    halves = mask_ref.shape[0]
    landed_refs, before_refs = refs[: halves - 1], refs[halves - 1 :]
    columns = chosen_ref.shape[1]
    rows = chosen_ref.shape[0] // halves
    summed = 0.0
    for h in range(halves):
        here = pl.ds(h * rows, rows)
        inputs = chosen_ref[here, :]
        for d, landed_ref in enumerate(landed_refs):
            landed = landed_ref[pl.ds((h ^ (d + 1)) * rows, rows), :]
            inputs = inputs + landed.astype(jnp.float32)
        total = total_ref[here, :]
        for before_ref in before_refs:
            total = total + before_ref[here, :]
        products = inputs * sum(
            total[:, d * columns : (d + 1) * columns] * mask_ref[d, here, :].astype(jnp.float32)
            for d in range(halves)
        )
        high = products.astype(jnp.bfloat16)
        low = (products - high.astype(jnp.float32)).astype(jnp.bfloat16)
        for part in (high, low):
            summed = summed + lax.dot_general(
                member_ref[here, :],
                part,
                (((0,), (0,)), ((), ())),
                preferred_element_type=jnp.float32,
            )
    scores = jnp.dot(
        summed,
        query_ref[...],
        precision=lax.Precision.HIGHEST,
        preferred_element_type=jnp.float32,
    )
    for i, out_ref in enumerate(out_refs):
        out_ref[...] = scores[i * SEG_DEV : (i + 1) * SEG_DEV]


def score_call(position, query_sum, extras, group, pieces, folds, layouts, aligned):
    total = sum(piece.shape[0] for piece in pieces)
    across = folds[0].shape[2]
    width = sum(fold.shape[0] * fold.shape[1] for fold in folds)
    slots = sum(fold.shape[0] for fold in folds)
    vmem, anywhere = pl.BlockSpec(memory_space=pltpu.VMEM), pl.BlockSpec(memory_space=pl.ANY)
    smem = pl.BlockSpec(memory_space=pltpu.SMEM)
    totals = jax.ShapeDtypeStruct((total, across), jnp.float32)
    semaphores = [
        pltpu.SemaphoreType.DMA((slots,)),
        pltpu.SemaphoreType.DMA((slots if aligned else 1, len(pieces))),
    ]
    buffers = [
        pltpu.VMEM((total, width), pieces[0].dtype),
        pltpu.VMEM((width, across), folds[0].dtype),
    ]
    options = dict(
        compiler_params=pltpu.CompilerParams(vmem_limit_bytes=58 * 1024 * 1024),
        cost_estimate=pl.CostEstimate(flops=1, bytes_accessed=1, transcendentals=0),
    )
    if not extras:
        return pl.pallas_call(
            functools.partial(first_kernel, layouts, len(pieces)),
            in_specs=[smem] + [anywhere] * (len(pieces) + len(folds)),
            out_specs=vmem,
            out_shape=totals,
            scratch_shapes=buffers + semaphores,
            **options,
        )(position, *pieces, *folds)
    scores = jax.ShapeDtypeStruct((SEG_DEV, query_sum.shape[1]), jnp.float32)
    return pl.pallas_call(
        functools.partial(last_kernel, layouts, aligned, len(pieces), len(extras), group),
        in_specs=[smem, vmem] + [anywhere] * (len(extras) + len(pieces) + len(folds)),
        out_specs=[vmem] * group,
        out_shape=[scores] * group,
        scratch_shapes=buffers
        + [pltpu.VMEM(totals.shape, jnp.float32)]
        + semaphores
        + [pltpu.SemaphoreType.DMA((len(extras),))]
        + [pltpu.VMEM(extra.shape, extra.dtype) for extra in extras],
        **options,
    )(position, query_sum, *extras, *pieces, *folds)


def output_layouts(orders):
    sides = [[], []]
    for n, order in enumerate(orders):
        relatives = slot_order(order)
        middle = len(relatives) // 2
        sides[0].append((relatives[:middle], n, len(orders)))
        sides[1].append((relatives[middle:], n, len(orders)))
    return sides


def per_device(
    activations,
    gate_gradient,
    routes,
    sequence_ids,
    input_basis,
    output_basis,
    input_query,
    output_query,
):
    blocks = lax.axis_size("dp")
    group = lax.axis_size("expert")
    halves = group // CORES
    place = lax.axis_index("dp")
    member = lax.axis_index("expert")
    half = member // CORES
    core = member % CORES
    tokens, top = routes.shape
    columns = input_query.shape[2]
    queries = columns // RANK
    count = bits_of(blocks)

    def send(packed, bit):
        return lax.ppermute(packed, "dp", flip(blocks, 1 << bit))

    def joined(keep, landed, exponent):
        half = (keep.shape[0] - TAIL) // 2
        there = landed[2 * half : 2 * half + 1].astype(jnp.float32)
        exponent = jnp.maximum(exponent, there) + 1
        packed = pack(keep, landed, there, exponent)
        here = slice(0, half + TAIL)
        values = landed[here].astype(jnp.float32) * jnp.exp2(there - TOP_EXPONENT)
        return packed, exponent, keep[here] + values

    def own_shard(keep, landed):
        rows = keep.shape[0] - TAIL
        there = landed[rows : rows + 1].astype(jnp.float32)
        values = landed[:rows].astype(jnp.float32) * jnp.exp2(there - TOP_EXPONENT)
        return (keep[:rows] + values).astype(jnp.bfloat16).reshape(halves, -1, columns)

    def exchange(shard):
        pieces = [shard[0]] + [
            lax.ppermute(shard[d], "expert", flip(group, d * CORES)) for d in range(1, halves)
        ]
        return jnp.concatenate(pieces, axis=1)

    def from_half(part, d):
        return part if d == 0 else lax.ppermute(part, "expert", flip(group, d * CORES))

    def from_core(part):
        return lax.ppermute(part, "expert", flip(group, 1))

    order_second = list(range(count))
    order_first = order_second[1::-1] + order_second[2:]
    position = jnp.stack([place, half, core]).astype(jnp.int32)

    def parts(bases, upper):
        queries = (input_query[0], output_query[0])
        return fold_parts(bases, queries, position, (order_first, order_second), halves, upper)

    bases = input_basis[0], output_basis[0]
    packed_first, packed_second = [part.astype(jnp.float16) for part in parts(bases, True)]
    *bases, activations, packed_first, packed_second = tie(
        *bases, activations, packed_first, packed_second
    )
    landed_first = send(packed_first, order_first[0])
    landed_second = send(packed_second, order_second[0])
    exponent_first = column_exponent(input_query[0])
    exponent_second = column_exponent(output_query[0])

    others = range(1, halves)
    gather_orders = [order_second, order_second[1:] + order_second[:1]]
    extra = jnp.concatenate([routes, sequence_ids.T], axis=1).astype(jnp.bfloat16)
    extra = jnp.pad(extra, ((0, 0), (0, columns - extra.shape[1])))
    input_parts = list(column_parts(activations, extra, position, halves))
    *bases, input_parts[0] = tie(*bases, input_parts[0])
    keep_first, keep_second = parts(bases, False)
    input_parts = [from_half(part, d) for d, part in enumerate(input_parts)]

    packed_first, exponent_first, keep_first = joined(keep_first, landed_first, exponent_first)
    landed_first = send(packed_first, order_first[1])
    packed_second, exponent_second, keep_second = joined(
        keep_second, landed_second, exponent_second
    )
    gate_gradient, packed_second = tie(gate_gradient, packed_second)
    landed_second = send(packed_second, order_second[1])
    own_gradient, early, late = flattened_parts(gate_gradient, position, halves)
    early = [from_half(part, d) for d, part in zip(others, early)]
    landed_first, own_gradient = tie(landed_first, own_gradient)

    for bit in order_first[2:]:
        packed_first, exponent_first, keep_first = joined(
            keep_first, landed_first, exponent_first
        )
        landed_first = send(packed_first, bit)
    for bit in order_second[2:]:
        packed_second, exponent_second, keep_second = joined(
            keep_second, landed_second, exponent_second
        )
        keep_second, landed_first = tie(keep_second, landed_first)
        landed_second = send(packed_second, bit)
    own_half, *input_parts = input_parts
    shard_first, *input_parts = tie(own_shard(keep_first, landed_first), *input_parts)
    input_pieces = [own_half, from_core(own_half)]
    for part in input_parts:
        input_pieces += [part, from_core(part)]
    swapped_gradient = from_core(own_gradient)
    mask, small_mask, membership = masks(position, input_pieces, top, halves, columns)
    query_sum = jnp.asarray(
        np.arange(columns)[:, None] // RANK == np.arange(queries)[None, :], jnp.float32
    )

    def split(shard):
        cut = (shard.shape[0] // len(gather_orders) + 15) // 16 * 16
        return [shard[:cut][None], shard[cut:][None]]

    def stage_of(held, stage):
        return [send(part, bits[stage]) for part, bits in zip(held, gather_orders)]

    def both(held, landed):
        return [jnp.concatenate(pair) for pair in zip(held, landed)]

    shard_first, *early = tie(shard_first, *early)
    swapped_early = [from_core(part) for part in early]
    shard_first = exchange(shard_first)
    shard_first, landed_second = tie(shard_first, landed_second)
    held_first = shard_first[None]
    landed_first = send(held_first, order_second[-1])
    shard_second = exchange(own_shard(keep_second, landed_second))
    shard_second, *late = tie(shard_second, *late)
    landed_first, mask, small_mask, membership, swapped_gradient, *swapped_early = tie(
        landed_first, mask, small_mask, membership, swapped_gradient, *swapped_early
    )
    held_first = jnp.concatenate([held_first, landed_first])
    late = [from_half(part, d) for d, part in zip(others, late)]
    held_second = split(shard_second)
    for stage in range(2, count):
        landed_first = send(held_first, order_second[-stage])
        landed = stage_of(held_second, 1 - stage)
        held_second = both(held_second, landed)
        landed_first, *held_second = tie(landed_first, *held_second)
        held_first = jnp.concatenate([held_first, landed_first])
    last_first = send(held_first, order_second[0])
    held_second = both(held_second, stage_of(held_second, 1 - count))
    last_second = stage_of(held_second, 0)
    last_first, *held_second = tie(last_first, *held_second)
    last_first, *late = tie(last_first, *late)

    chosen, sent = input_chosen(
        position, input_pieces, [held_first, last_first], [order_second], mask, top
    )
    pieces = [own_gradient, swapped_gradient]
    for first_part, last_part, swapped_part in zip(early, late, swapped_early):
        pieces += [first_part, last_part, swapped_part, from_core(last_part)]
    layouts = output_layouts(gather_orders)
    aligned = held_second[0].shape[1] % 128 == 0
    before = []
    if aligned:
        sent, *held_second = tie(sent, *held_second)
        before = [
            score_call(
                position, query_sum, [], group, pieces, held_second, layouts[0], aligned
            )
        ]
        held_second, layouts = last_second, layouts[1]
    else:
        held_second, layouts = held_second + last_second, layouts[0] + layouts[1]
    landed = [lax.ppermute(sent, "expert", flip(group, d * CORES)) for d in others]
    partial = score_call(
        position,
        query_sum,
        [small_mask, membership, chosen, *landed, *before],
        group,
        pieces,
        held_second,
        layouts,
        aligned,
    )
    scores = partial[0]
    for d in range(1, group):
        scores = scores + lax.ppermute(partial[d], "expert", flip(group, d))
    return scores


def solution(mesh):
    return jax.shard_map(
        per_device,
        mesh=mesh,
        in_specs=(
            P(("dp", "expert"), None),
            P(("dp", "expert"), None, None),
            P(("dp", "expert"), None),
            P(("dp", "expert"), None),
            P("expert", None, "dp"),
            P("expert", None, "dp"),
            P("expert", "dp", None),
            P("expert", "dp", None),
        ),
        out_specs=P(("dp", "expert"), None),
        check_vma=False,
    )
```

```python
import functools

import jax
import jax.numpy as jnp
import numpy as np
from jax import lax
from jax.experimental import pallas as pl
from jax.experimental.pallas import tpu as pltpu
from jax.sharding import PartitionSpec as P

RANK = 32
SEG_DEV = 4
CORES = 2
TOP_EXPONENT = 15.0
TAIL = 16


def bits_of(count):
    return (count - 1).bit_length()


def slot_order(order):
    width = len(order)
    return [
        sum(((slot >> (width - 1 - i)) & 1) << bit for i, bit in enumerate(order))
        for slot in range(1 << width)
    ]


def column_exponent(query):
    peak = jnp.max(jnp.abs(query).astype(jnp.float32), axis=0, keepdims=True)
    bound = jnp.maximum(peak * (0.25 * query.shape[0]), 1e-28)
    return jnp.floor(jnp.log2(bound)) + 1.0


def fold_kernel(width, steps, scaled, *refs):
    basis_refs, refs = refs[1 : 1 + 2 * width], refs[1 + 2 * width :]
    query_refs, out_refs, sum_refs, done = refs[:2], refs[2:4], refs[4:6], refs[6]
    step = pl.program_id(0)
    for chunk in range(2):
        query_ref, out_ref, sum_ref = query_refs[chunk], out_refs[chunk], sum_refs[chunk]
        chunk_refs = basis_refs[chunk * width : (chunk + 1) * width]
        rows = chunk_refs[0].shape[0]

        def piece(index):
            here = pl.ds(index * (width * rows), width * rows)
            return pltpu.make_async_copy(
                sum_ref.at[here, :], out_ref.at[here, :], done.at[chunk, index]
            )

        here = pl.ds(steps * width * rows, TAIL)
        tail = pltpu.make_async_copy(
            sum_ref.at[here, :], out_ref.at[here, :], done.at[chunk, steps]
        )
        for index in range(steps):

            @pl.when(step == chunk * steps + index)
            def _():
                exponent = column_exponent(query_ref[...])
                for part, basis_ref in enumerate(chunk_refs):
                    terms = jnp.dot(
                        basis_ref[...], query_ref[...], preferred_element_type=jnp.float32
                    )
                    if scaled:
                        terms = terms * jnp.exp2(TOP_EXPONENT - exponent)
                    sum_ref[pl.ds((index * width + part) * rows, rows), :] = terms
                piece(index).start()
                if index == 0:
                    sum_ref[here, :] = jnp.broadcast_to(exponent, (TAIL, sum_ref.shape[1]))
                    tail.start()

        @pl.when(step == 2 * steps - 1)
        def _():
            for index in range(steps):
                piece(index).wait()
            tail.wait()


def fold_parts(bases, queries, position, orders, halves, upper):
    columns = queries[0].shape[1]
    blocks = 1 << len(orders[0])
    count = blocks * halves
    width = min(4, count // 2)
    steps = count // 2 // width

    def block(chunk, part):
        order, basis = orders[chunk], bases[chunk]

        def index(i, position_ref):
            i = jnp.clip(i - chunk * steps, 0, steps - 1)
            slot = (i * width + part) // halves + (blocks // 2 if upper else 0)
            relative = sum(
                ((slot >> (len(order) - 1 - n)) & 1) << bit for n, bit in enumerate(order)
            )
            here = (i * width + part) % halves ^ position_ref[1]
            return here * blocks + (relative ^ position_ref[0]), 0

        return pl.BlockSpec((basis.shape[0] // count, basis.shape[1]), index)

    out_shape = [
        jax.ShapeDtypeStruct((basis.shape[0] // 2 + TAIL, columns), jnp.float32)
        for basis in bases
    ]
    return pl.pallas_call(
        functools.partial(fold_kernel, width, steps, upper),
        grid_spec=pltpu.PrefetchScalarGridSpec(
            num_scalar_prefetch=1,
            grid=(2 * steps,),
            in_specs=[block(chunk, part) for chunk in range(2) for part in range(width)]
            + [pl.BlockSpec(query.shape, lambda i, p: (0, 0)) for query in queries],
            out_specs=[pl.BlockSpec(memory_space=pl.ANY)] * 2,
            scratch_shapes=[pltpu.VMEM(out.shape, out.dtype) for out in out_shape]
            + [pltpu.SemaphoreType.DMA((2, steps + 1))],
        ),
        out_shape=out_shape,
        compiler_params=pltpu.CompilerParams(vmem_limit_bytes=56 * 1024 * 1024),
        cost_estimate=pl.CostEstimate(flops=1, bytes_accessed=1, transcendentals=0),
    )(position, *([bases[0]] * width), *([bases[1]] * width), *queries)


def pack(keep, landed, there, exponent):
    half = (keep.shape[0] - TAIL) // 2
    values = landed[half:].astype(jnp.float32) * jnp.exp2(there - TOP_EXPONENT)
    scaled = (keep[half:] + values) * jnp.exp2(TOP_EXPONENT - exponent)
    row = lax.broadcasted_iota(jnp.int32, scaled.shape, 0)
    return jnp.where(row < half, scaled, exponent).astype(jnp.float16)


def flip(size, mask):
    return [(i, i ^ mask) for i in range(size)]


def tie(*values):
    return lax.optimization_barrier(values)


def column_kernel(halves, position_ref, source_ref, extra_ref, *out_refs):
    width = source_ref.shape[1]
    for d in range(halves):

        @pl.when(pl.program_id(0) == d)
        def _():
            out_refs[d][:, pl.ds(0, width)] = source_ref[...]
            out_refs[d][:, pl.ds(width, extra_ref.shape[1])] = extra_ref[...]


def column_parts(source, extra, position, halves):
    rows, width = source.shape[0], source.shape[1] // halves
    out_shape = (rows, width + extra.shape[1])
    return pl.pallas_call(
        functools.partial(column_kernel, halves),
        grid_spec=pltpu.PrefetchScalarGridSpec(
            num_scalar_prefetch=1,
            grid=(halves,),
            in_specs=[
                pl.BlockSpec((rows, width), lambda j, p: (0, p[1] ^ j)),
                pl.BlockSpec(extra.shape, lambda j, p: (0, 0)),
            ],
            out_specs=[pl.BlockSpec(out_shape, lambda j, p: (0, 0))] * halves,
        ),
        out_shape=[jax.ShapeDtypeStruct(out_shape, source.dtype)] * halves,
        compiler_params=pltpu.CompilerParams(vmem_limit_bytes=56 * 1024 * 1024),
        cost_estimate=pl.CostEstimate(flops=1, bytes_accessed=1, transcendentals=0),
    )(position, source, extra)


def flatten_kernel(halves, position_ref, source_ref, *out_refs):
    step = pl.program_id(0)
    rows, width = out_refs[0].shape
    for d in range(halves):
        start = pl.multiple_of((position_ref[1] ^ d) * width, width)
        part = source_ref[:, :, pl.ds(start, width)].reshape(rows, width)
        if d == 0:
            out_refs[0][...] = part
            continue

        @pl.when(step == 0)
        def _():
            out_refs[2 * d - 1][...] = part

        @pl.when(step > 0)
        def _():
            out_refs[2 * d][...] = part


def flattened_parts(source, position, halves):
    tokens, top, width = source.shape
    block = 32
    rows, width = block * top, width // halves
    shapes = [tokens * top] + [rows, tokens * top - rows] * (halves - 1)
    specs = [
        pl.BlockSpec((rows, width), lambda i, p: (i, 0)),
        pl.BlockSpec((rows, width), lambda i, p: (0, 0)),
        pl.BlockSpec((rows, width), lambda i, p: (jnp.maximum(i - 1, 0), 0)),
    ]
    own, *away = pl.pallas_call(
        functools.partial(flatten_kernel, halves),
        grid_spec=pltpu.PrefetchScalarGridSpec(
            num_scalar_prefetch=1,
            grid=(tokens // block,),
            in_specs=[pl.BlockSpec((block,) + source.shape[1:], lambda i, p: (i, 0, 0))],
            out_specs=specs[:1] + specs[1:] * (halves - 1),
        ),
        out_shape=[jax.ShapeDtypeStruct((count, width), source.dtype) for count in shapes],
        compiler_params=pltpu.CompilerParams(vmem_limit_bytes=56 * 1024 * 1024),
        cost_estimate=pl.CostEstimate(
            flops=1, bytes_accessed=4 * source.size, transcendentals=0
        ),
    )(position, source)
    return own, away[0::2], away[1::2]


def start_all(copies, done):
    started = []
    for i, (source, target) in enumerate(copies):
        started.append(pltpu.make_async_copy(source, target, done.at[i]))
        started[i].start()
    return started


def mask_kernel(top, position_ref, *refs):
    *extra_refs, mask_ref, small_mask_ref, member_ref, rows_ref = refs
    tokens, lanes = extra_refs[0].shape
    lane = lax.broadcasted_iota(jnp.int32, (tokens, lanes), 1).astype(jnp.float32)
    for i, extra_ref in enumerate(extra_refs):
        extra = extra_ref[...].astype(jnp.float32)

        def column(k):
            return jnp.broadcast_to(extra[:, k : k + 1], (tokens, lanes))

        member = jnp.where(column(top) + float(i * SEG_DEV) == lane, 1.0, 0.0)
        for k in range(top):
            rows = pl.ds(i * tokens * top + k, tokens, stride=top)
            rows_ref[rows, :] = member
            for d in range(mask_ref.shape[0]):
                expert = ((position_ref[1] ^ d) * CORES + position_ref[2]).astype(jnp.float32)
                mask_ref[d, rows, :] = jnp.where(column(k) == expert, 1.0, 0.0)
    member_ref[...] = rows_ref[...].astype(member_ref.dtype)
    small_mask_ref[...] = mask_ref[...].astype(small_mask_ref.dtype)


def masks(position, pieces, top, halves, lanes):
    tokens = pieces[0].shape[0]
    rows = len(pieces) * tokens * top
    last = pieces[0].shape[1] // lanes - 1
    return pl.pallas_call(
        functools.partial(mask_kernel, top),
        grid=(1,),
        in_specs=[pl.BlockSpec(memory_space=pltpu.SMEM)]
        + [pl.BlockSpec((tokens, lanes), lambda i: (0, last))] * len(pieces),
        out_specs=[
            pl.BlockSpec((halves, rows, lanes), lambda i: (0, 0, 0)),
            pl.BlockSpec((halves, rows, lanes), lambda i: (0, 0, 0)),
            pl.BlockSpec((rows, lanes), lambda i: (0, 0)),
        ],
        out_shape=[
            jax.ShapeDtypeStruct((halves, rows, lanes), jnp.float32),
            jax.ShapeDtypeStruct((halves, rows, lanes), jnp.bfloat16),
            jax.ShapeDtypeStruct((rows, lanes), jnp.bfloat16),
        ],
        scratch_shapes=[pltpu.VMEM((rows, lanes), jnp.float32)],
        cost_estimate=pl.CostEstimate(flops=1, bytes_accessed=60000000, transcendentals=0),
    )(position, *pieces)


def input_kernel(top, layouts, count, position_ref, mask_in_ref, *refs):
    *refs, out_ref, sent_ref, tokens_ref, held_ref, mask_ref, done = refs
    token_refs, fold_refs = refs[:count], refs[count:]
    rows = token_refs[0].shape[0]
    copies = [
        (token_ref.at[:, pl.ds(0, tokens_ref.shape[1])], tokens_ref.at[pl.ds(i * rows, rows), :])
        for i, token_ref in enumerate(token_refs)
    ]
    for fold_ref, (relatives, offset, block) in zip(fold_refs, layouts):
        rows = fold_ref.shape[1]
        for slot, relative in enumerate(relatives):
            start = pl.multiple_of((relative ^ position_ref[0]) * block + offset, 16)
            copies.append((fold_ref.at[slot], held_ref.at[pl.ds(start, rows), :]))
    *copies, mask_copy = start_all(copies + [(mask_in_ref, mask_ref)], done)
    for copy in copies:
        copy.wait()
    terms = jnp.dot(tokens_ref[...], held_ref[...], preferred_element_type=jnp.float32)
    mask_copy.wait()
    total = tokens_ref.shape[0]
    columns = out_ref.shape[1]
    for k in range(top):
        rows_of = pl.ds(k, total, stride=top)
        out_ref[rows_of, :] = sum(
            terms[:, d * columns : (d + 1) * columns] * mask_ref[d, rows_of, :]
            for d in range(mask_ref.shape[0])
        )
    sent_ref[...] = out_ref[...].astype(sent_ref.dtype)


def input_chosen(position, pieces, held, orders, mask, top):
    total = sum(piece.shape[0] for piece in pieces)
    columns = mask.shape[2]
    width, across = pieces[0].shape[1] - columns, held[0].shape[2]
    block = sum(part.shape[1] for part in held[0::2])
    layouts, offset = [], 0
    for first, last, order in zip(held[0::2], held[1::2], orders):
        relatives = slot_order(order)
        middle = first.shape[0]
        layouts += [(relatives[:middle], offset, block), (relatives[middle:], offset, block)]
        offset += first.shape[1]
    slots = sum(part.shape[0] for part in held)
    return pl.pallas_call(
        functools.partial(input_kernel, top, layouts, len(pieces)),
        in_specs=[pl.BlockSpec(memory_space=pltpu.SMEM)]
        + [pl.BlockSpec(memory_space=pl.ANY)] * (1 + len(pieces) + len(held)),
        out_specs=[pl.BlockSpec(memory_space=pltpu.VMEM)] * 2,
        out_shape=[
            jax.ShapeDtypeStruct((total * top, columns), jnp.float32),
            jax.ShapeDtypeStruct((total * top, columns), jnp.bfloat16),
        ],
        scratch_shapes=[
            pltpu.VMEM((total, width), pieces[0].dtype),
            pltpu.VMEM((width, across), held[0].dtype),
            pltpu.VMEM(mask.shape, mask.dtype),
            pltpu.SemaphoreType.DMA((len(pieces) + slots + 1,)),
        ],
        compiler_params=pltpu.CompilerParams(vmem_limit_bytes=58 * 1024 * 1024),
        cost_estimate=pl.CostEstimate(flops=1, bytes_accessed=1, transcendentals=0),
    )(position, mask, *pieces, *held)


def spans(counts):
    starts = [sum(counts[:i]) for i in range(len(counts))]
    return list(zip(starts, counts))


def output_terms(position_ref, layouts, aligned, token_refs, fold_refs, buffers):
    tokens_ref, fold_ref, total_ref, folded, done = buffers
    counts = [token_ref.shape[0] for token_ref in token_refs]
    fold_copies, token_copies, row = [], [], 0
    for held_ref, (relatives, part, size) in zip(fold_refs, layouts):
        rows = held_ref.shape[1]
        for slot, relative in enumerate(relatives):
            block = (relative ^ position_ref[0]) * size + part
            target = row if aligned else pl.multiple_of(block * rows, rows)
            fold_copies.append((held_ref.at[slot], fold_ref.at[pl.ds(target, rows), :]))
            if aligned:
                across = pl.ds(row, rows)
                token_copies.append(
                    [
                        (
                            token_ref.at[:, pl.ds(pl.multiple_of(block * rows, rows), rows)],
                            tokens_ref.at[pl.ds(first, count), across],
                        )
                        for token_ref, (first, count) in zip(token_refs, spans(counts))
                    ]
                )
            row += rows
    if not aligned:
        token_copies = [
            [
                (token_ref, tokens_ref.at[pl.ds(first, count), :])
                for token_ref, (first, count) in zip(token_refs, spans(counts))
            ]
        ]
    fold_copies = start_all(fold_copies, folded)
    token_copies = [start_all(copies, done.at[i]) for i, copies in enumerate(token_copies)]
    for copy in fold_copies:
        copy.wait()
    for copies in token_copies:
        for copy in copies:
            copy.wait()
    total_ref[...] = jnp.dot(
        tokens_ref[...], fold_ref[...], preferred_element_type=jnp.float32
    )


def first_kernel(layouts, count, position_ref, *refs):
    token_refs, refs = refs[:count], refs[count:]
    *fold_refs, total_ref, tokens_ref, fold_ref, folded, done = refs
    buffers = tokens_ref, fold_ref, total_ref, folded, done
    output_terms(position_ref, layouts, True, token_refs, fold_refs, buffers)


def last_kernel(layouts, aligned, count, extra_count, group, position_ref, *refs):
    query_ref, *refs = refs
    extra_refs, refs = refs[:extra_count], refs[extra_count:]
    token_refs, refs = refs[:count], refs[count:]
    held_refs, refs = refs[-extra_count:], refs[:-extra_count]
    fold_refs, refs = refs[: len(layouts)], refs[len(layouts) :]
    out_refs, (tokens_ref, fold_ref, total_ref, folded, done, extra_done) = refs[:group], refs[group:]
    extra_copies = start_all(list(zip(extra_refs, held_refs)), extra_done)
    buffers = tokens_ref, fold_ref, total_ref, folded, done
    output_terms(position_ref, layouts, aligned, token_refs, fold_refs, buffers)
    for copy in extra_copies:
        copy.wait()
    mask_ref, member_ref, chosen_ref, *refs = held_refs
    halves = mask_ref.shape[0]
    landed_refs, before_refs = refs[: halves - 1], refs[halves - 1 :]
    columns = chosen_ref.shape[1]
    rows = chosen_ref.shape[0] // halves
    summed = 0.0
    for h in range(halves):
        here = pl.ds(h * rows, rows)
        inputs = chosen_ref[here, :]
        for d, landed_ref in enumerate(landed_refs):
            landed = landed_ref[pl.ds((h ^ (d + 1)) * rows, rows), :]
            inputs = inputs + landed.astype(jnp.float32)
        total = total_ref[here, :]
        for before_ref in before_refs:
            total = total + before_ref[here, :]
        products = inputs * sum(
            total[:, d * columns : (d + 1) * columns] * mask_ref[d, here, :].astype(jnp.float32)
            for d in range(halves)
        )
        high = products.astype(jnp.bfloat16)
        low = (products - high.astype(jnp.float32)).astype(jnp.bfloat16)
        for part in (high, low):
            summed = summed + lax.dot_general(
                member_ref[here, :],
                part,
                (((0,), (0,)), ((), ())),
                preferred_element_type=jnp.float32,
            )
    scores = jnp.dot(
        summed,
        query_ref[...],
        precision=lax.Precision.HIGHEST,
        preferred_element_type=jnp.float32,
    )
    for i, out_ref in enumerate(out_refs):
        out_ref[...] = scores[i * SEG_DEV : (i + 1) * SEG_DEV]


def score_call(position, query_sum, extras, group, pieces, folds, layouts, aligned):
    total = sum(piece.shape[0] for piece in pieces)
    across = folds[0].shape[2]
    width = sum(fold.shape[0] * fold.shape[1] for fold in folds)
    slots = sum(fold.shape[0] for fold in folds)
    vmem, anywhere = pl.BlockSpec(memory_space=pltpu.VMEM), pl.BlockSpec(memory_space=pl.ANY)
    smem = pl.BlockSpec(memory_space=pltpu.SMEM)
    totals = jax.ShapeDtypeStruct((total, across), jnp.float32)
    semaphores = [
        pltpu.SemaphoreType.DMA((slots,)),
        pltpu.SemaphoreType.DMA((slots if aligned else 1, len(pieces))),
    ]
    buffers = [
        pltpu.VMEM((total, width), pieces[0].dtype),
        pltpu.VMEM((width, across), folds[0].dtype),
    ]
    options = dict(
        compiler_params=pltpu.CompilerParams(vmem_limit_bytes=32 * 1024 * 1024),
        cost_estimate=pl.CostEstimate(flops=1, bytes_accessed=1, transcendentals=0),
    )
    if not extras:
        return pl.pallas_call(
            functools.partial(first_kernel, layouts, len(pieces)),
            in_specs=[smem] + [anywhere] * (len(pieces) + len(folds)),
            out_specs=vmem,
            out_shape=totals,
            scratch_shapes=buffers + semaphores,
            **options,
        )(position, *pieces, *folds)
    scores = jax.ShapeDtypeStruct((SEG_DEV, query_sum.shape[1]), jnp.float32)
    return pl.pallas_call(
        functools.partial(last_kernel, layouts, aligned, len(pieces), len(extras), group),
        in_specs=[smem, vmem] + [anywhere] * (len(extras) + len(pieces) + len(folds)),
        out_specs=[vmem] * group,
        out_shape=[scores] * group,
        scratch_shapes=buffers
        + [pltpu.VMEM(totals.shape, jnp.float32)]
        + semaphores
        + [pltpu.SemaphoreType.DMA((len(extras),))]
        + [pltpu.VMEM(extra.shape, extra.dtype) for extra in extras],
        **options,
    )(position, query_sum, *extras, *pieces, *folds)


def output_layouts(orders):
    sides = [[], []]
    for n, order in enumerate(orders):
        relatives = slot_order(order)
        middle = len(relatives) // 2
        sides[0].append((relatives[:middle], n, len(orders)))
        sides[1].append((relatives[middle:], n, len(orders)))
    return sides


def per_device(
    activations,
    gate_gradient,
    routes,
    sequence_ids,
    input_basis,
    output_basis,
    input_query,
    output_query,
):
    blocks = lax.axis_size("dp")
    group = lax.axis_size("expert")
    halves = group // CORES
    place = lax.axis_index("dp")
    member = lax.axis_index("expert")
    half = member // CORES
    core = member % CORES
    tokens, top = routes.shape
    columns = input_query.shape[2]
    queries = columns // RANK
    count = bits_of(blocks)

    def send(packed, bit):
        return lax.ppermute(packed, "dp", flip(blocks, 1 << bit))

    def joined(keep, landed, exponent):
        half = (keep.shape[0] - TAIL) // 2
        there = landed[2 * half : 2 * half + 1].astype(jnp.float32)
        exponent = jnp.maximum(exponent, there) + 1
        packed = pack(keep, landed, there, exponent)
        here = slice(0, half + TAIL)
        values = landed[here].astype(jnp.float32) * jnp.exp2(there - TOP_EXPONENT)
        return packed, exponent, keep[here] + values

    def own_shard(keep, landed):
        rows = keep.shape[0] - TAIL
        there = landed[rows : rows + 1].astype(jnp.float32)
        values = landed[:rows].astype(jnp.float32) * jnp.exp2(there - TOP_EXPONENT)
        return (keep[:rows] + values).astype(jnp.bfloat16).reshape(halves, -1, columns)

    def exchange(shard):
        pieces = [shard[0]] + [
            lax.ppermute(shard[d], "expert", flip(group, d * CORES)) for d in range(1, halves)
        ]
        return jnp.concatenate(pieces, axis=1)

    def from_half(part, d):
        return part if d == 0 else lax.ppermute(part, "expert", flip(group, d * CORES))

    def from_core(part):
        return lax.ppermute(part, "expert", flip(group, 1))

    order_second = list(range(count))
    order_first = order_second[1::-1] + order_second[2:]
    position = jnp.stack([place, half, core]).astype(jnp.int32)

    def parts(bases, upper):
        queries = (input_query[0], output_query[0])
        return fold_parts(bases, queries, position, (order_first, order_second), halves, upper)

    bases = input_basis[0], output_basis[0]
    packed_first, packed_second = [part.astype(jnp.float16) for part in parts(bases, True)]
    *bases, activations, packed_first, packed_second = tie(
        *bases, activations, packed_first, packed_second
    )
    landed_first = send(packed_first, order_first[0])
    landed_second = send(packed_second, order_second[0])
    exponent_first = column_exponent(input_query[0])
    exponent_second = column_exponent(output_query[0])

    others = range(1, halves)
    gather_orders = [order_second, order_second[1:] + order_second[:1]]
    extra = jnp.concatenate([routes, sequence_ids.T], axis=1).astype(jnp.bfloat16)
    extra = jnp.pad(extra, ((0, 0), (0, columns - extra.shape[1])))
    input_parts = list(column_parts(activations, extra, position, halves))
    *bases, input_parts[0] = tie(*bases, input_parts[0])
    keep_first, keep_second = parts(bases, False)
    input_parts = [from_half(part, d) for d, part in enumerate(input_parts)]

    packed_first, exponent_first, keep_first = joined(keep_first, landed_first, exponent_first)
    landed_first = send(packed_first, order_first[1])
    packed_second, exponent_second, keep_second = joined(
        keep_second, landed_second, exponent_second
    )
    gate_gradient, packed_second = tie(gate_gradient, packed_second)
    landed_second = send(packed_second, order_second[1])
    own_gradient, early, late = flattened_parts(gate_gradient, position, halves)
    early = [from_half(part, d) for d, part in zip(others, early)]
    landed_first, own_gradient = tie(landed_first, own_gradient)

    for bit in order_first[2:]:
        packed_first, exponent_first, keep_first = joined(
            keep_first, landed_first, exponent_first
        )
        landed_first = send(packed_first, bit)
    for bit in order_second[2:]:
        packed_second, exponent_second, keep_second = joined(
            keep_second, landed_second, exponent_second
        )
        keep_second, landed_first = tie(keep_second, landed_first)
        landed_second = send(packed_second, bit)
    own_half, *input_parts = input_parts
    shard_first, *input_parts = tie(own_shard(keep_first, landed_first), *input_parts)
    input_pieces = [own_half, from_core(own_half)]
    for part in input_parts:
        input_pieces += [part, from_core(part)]
    swapped_gradient = from_core(own_gradient)
    query_sum = jnp.asarray(
        np.arange(columns)[:, None] // RANK == np.arange(queries)[None, :], jnp.float32
    )

    def split(shard):
        cut = (shard.shape[0] // len(gather_orders) + 15) // 16 * 16
        return [shard[:cut][None], shard[cut:][None]]

    def stage_of(held, stage):
        return [send(part, bits[stage]) for part, bits in zip(held, gather_orders)]

    def both(held, landed):
        return [jnp.concatenate(pair) for pair in zip(held, landed)]

    shard_first, *early = tie(shard_first, *early)
    swapped_early = [from_core(part) for part in early]
    shard_first = exchange(shard_first)
    shard_first, landed_second = tie(shard_first, landed_second)
    held_first = shard_first[None]
    landed_first = send(held_first, order_second[-1])
    shard_second = exchange(own_shard(keep_second, landed_second))
    shard_second, *rest = tie(shard_second, *late, *input_pieces)
    late, input_pieces = rest[: halves - 1], rest[halves - 1 :]
    landed_first, swapped_gradient, *swapped_early = tie(
        landed_first, swapped_gradient, *swapped_early
    )
    held_first = jnp.concatenate([held_first, landed_first])
    late = [from_half(part, d) for d, part in zip(others, late)]
    held_second = split(shard_second)
    for stage in range(2, count):
        landed_first = send(held_first, order_second[-stage])
        landed = stage_of(held_second, 1 - stage)
        held_second = both(held_second, landed)
        if stage + 1 == count:
            input_pieces[0], *rest = tie(input_pieces[0], *held_second)
            mask, small_mask, membership = masks(position, input_pieces, top, halves, columns)
            landed_first, mask, small_mask, membership, *rest = tie(
                landed_first, mask, small_mask, membership, *rest
            )
        held_first = jnp.concatenate([held_first, landed_first])
    last_first = send(held_first, order_second[0])
    held_second = both(rest, stage_of(held_second, 1 - count))
    last_second = stage_of(held_second, 0)
    last_first, *held_second = tie(last_first, *held_second)
    last_first, *late = tie(last_first, *late)

    chosen, sent = input_chosen(
        position, input_pieces, [held_first, last_first], [order_second], mask, top
    )
    pieces = [own_gradient, swapped_gradient]
    for first_part, last_part, swapped_part in zip(early, late, swapped_early):
        pieces += [first_part, last_part, swapped_part, from_core(last_part)]
    layouts = output_layouts(gather_orders)
    aligned = held_second[0].shape[1] % 128 == 0
    before = []
    if aligned:
        sent, *held_second = tie(sent, *held_second)
        before = [
            score_call(
                position, query_sum, [], group, pieces, held_second, layouts[0], aligned
            )
        ]
        held_second, layouts = last_second, layouts[1]
    else:
        held_second, layouts = held_second + last_second, layouts[0] + layouts[1]
    landed = [lax.ppermute(sent, "expert", flip(group, d * CORES)) for d in others]
    partial = score_call(
        position,
        query_sum,
        [small_mask, membership, chosen, *landed, *before],
        group,
        pieces,
        held_second,
        layouts,
        aligned,
    )
    scores = partial[0]
    for d in range(1, group):
        scores = scores + lax.ppermute(partial[d], "expert", flip(group, d))
    return scores


def solution(mesh):
    return jax.shard_map(
        per_device,
        mesh=mesh,
        in_specs=(
            P(("dp", "expert"), None),
            P(("dp", "expert"), None, None),
            P(("dp", "expert"), None),
            P(("dp", "expert"), None),
            P("expert", None, "dp"),
            P("expert", None, "dp"),
            P("expert", "dp", None),
            P("expert", "dp", None),
        ),
        out_specs=P(("dp", "expert"), None),
        check_vma=False,
    )
```
